128 devices in a mesh: row: 16 (over z, x), col: 8 (over y, core).
Axes of the slice: x: 4, y: 4, z: 4, core: 2. Of those that a mesh axis runs over, the one named last changes fastest.
Arguments:
- histograms: bfloat16 [256, 640, 672], P(('row', 'col')), as said below
- basis: bfloat16 [256, 32, 640], P(('row', 'col')), may hold values from -6 to 6
- row_pairs: int32 [128, 16, 2], P(('row', 'col')), may hold values from -1 to 1, as said below
- col_pairs: int32 [128, 8, 2], P(('row', 'col')), may hold values from -1 to 1, as said below
Outputs:
- product: float32 [256, 32, 640], P(('row', 'col'))
The draws below stay inside these ranges and needn't reach their ends.
Inputs may be any that keep to these rules, and one draw needn't show every extreme that they name: histograms entries are nonnegative. row_pairs[d, s] concerns the device at row s in the column of device d: (own local block, partner local block on that device), or (-1, -1) where device d takes no pair with it, always so at s equal to d's own row; for two devices at most one lists the other, so every pair stands once. col_pairs[d, s] concerns the device at column s in the row of device d, with the same meaning and the same rules.
All inputs are finite; a program needn't handle non-finite values.
Results may differ from the reference program's by a relative error of at most 0.0028.
Values may be sent and summed in bfloat16 or wider, within the bound.
A program may use at most 192 MiB of HBM per device.

```python
import jax
import jax.numpy as jnp
from jax import lax

TYPES = 21
BINS = 32
F = 672
BS = 640
COLS = 32
BLK_DEV = 2
ROW_DEVS = 16
COL_DEVS = 8
NBLK = 256


def device_weights(key):
    return jax.random.randint(jax.random.fold_in(key, 5), (ROW_DEVS, COL_DEVS), 1, 9)


def orient_links(key, weights, peers):
    link_key, toss_key, chosen_key = jax.random.split(key, 3)
    groups = weights.shape[0]
    link_draw = jax.random.randint(link_key, (groups, peers, peers), 0, 10)
    toss_draw = jax.random.randint(toss_key, (groups, peers, peers), 0, 1 << 20)
    chosen = jax.random.randint(chosen_key, (groups, peers, peers), 0, BLK_DEV)
    first_ids = jnp.arange(peers)[:, None]
    second_ids = jnp.arange(peers)[None, :]
    upper = first_ids < second_ids
    link_sym = jnp.where(upper[None], link_draw, jnp.swapaxes(link_draw, 1, 2))
    toss_sym = jnp.where(upper[None], toss_draw, jnp.swapaxes(toss_draw, 1, 2))
    weight_first = weights[:, :, None]
    weight_second = weights[:, None, :]
    remainder = toss_sym % (weight_first + weight_second)
    mine = jnp.where(upper[None], remainder < weight_first, remainder >= weight_second)
    computes = (link_sym < 9) & (first_ids != second_ids)[None] & mine
    own_block = jnp.where(computes, chosen, -1)
    partner_block = jnp.where(computes, jnp.swapaxes(chosen, 1, 2), -1)
    return jnp.stack([own_block, partner_block], axis=-1).astype(jnp.int32)


def draw_row_pairs(key, part):
    weights = device_weights(key)
    key = jax.random.fold_in(key, 21)
    table = orient_links(key, weights.T, ROW_DEVS)
    return jnp.transpose(table, (1, 0, 2, 3)).reshape(ROW_DEVS * COL_DEVS, ROW_DEVS, 2)


def draw_col_pairs(key, part):
    weights = device_weights(key)
    key = jax.random.fold_in(key, 33)
    table = orient_links(key, weights, COL_DEVS)
    return table.reshape(ROW_DEVS * COL_DEVS, COL_DEVS, 2)


def draw_histograms(key, part):
    key = jax.random.fold_in(key, 11)
    amount_key, spread_key = jax.random.split(key)
    amount = jax.random.uniform(amount_key, (NBLK, BS, TYPES, 1), jnp.float32)
    spread = jax.random.uniform(spread_key, (NBLK, BS, TYPES, BINS), jnp.float32, 0.25, 1.75)
    return (amount * spread).reshape(NBLK, BS, TYPES * BINS).astype(jnp.bfloat16)


def levels(stream_key, dims, cuts, low, largest):
    gain = 1.0
    for axis_at, parts in cuts:
        heights = jax.random.uniform(jax.random.fold_in(jax.random.fold_in(stream_key, 6), axis_at), (parts,), jnp.float32, low / len(cuts), largest / len(cuts))
        gain = gain * jnp.repeat(jnp.exp(heights), dims[axis_at] // parts).reshape((-1,) + (1,) * (len(dims) - 1 - axis_at))
    return gain


def noise(stream_key, extent, width, limit, cuts=(), kind=jnp.bfloat16):
    values = width * jax.random.normal(stream_key, extent, jnp.float32)
    if cuts:
        values = values * levels(stream_key, extent, cuts, -0.22, 0.18)
    return jnp.clip(values, -limit, limit).astype(kind)


def setup_inputs(seed: int = 0) -> dict:
    splits = jax.random.split(jax.random.key(seed), 5)
    histograms = draw_histograms(jax.random.fold_in(splits[4], 71), 0)
    basis = noise(splits[1], (NBLK, COLS, BS), 1.0, 6.0, ((0, 128),))
    row_pairs = draw_row_pairs(jax.random.fold_in(splits[4], 71), 0)
    col_pairs = draw_col_pairs(jax.random.fold_in(splits[4], 71), 0)
    return {"histograms": histograms, "basis": basis, "row_pairs": row_pairs, "col_pairs": col_pairs}


def kernel_tile(first_rows, second_rows):
    first_sq = jnp.sum(jnp.square(first_rows.astype(jnp.float32)), axis=1)
    second_sq = jnp.sum(jnp.square(second_rows.astype(jnp.float32)), axis=1)
    inner_products = jnp.dot(first_rows, second_rows.T, preferred_element_type=jnp.float32)
    distances = first_sq[:, None] + second_sq[None, :] - 2.0 * inner_products
    return jnp.exp(-jnp.maximum(distances, 0.0) / (0.09 * F)).astype(jnp.bfloat16)


def reference(histograms, basis, row_pairs, col_pairs):
    def diagonal_term(block_id):
        kernel = kernel_tile(histograms[block_id], histograms[block_id])
        return jnp.dot(basis[block_id], kernel, preferred_element_type=jnp.float32)

    product = lax.map(diagonal_term, jnp.arange(NBLK, dtype=jnp.int32))
    device_ids = jnp.arange(ROW_DEVS * COL_DEVS, dtype=jnp.int32)
    row_of = device_ids // COL_DEVS
    col_of = device_ids % COL_DEVS
    row_first = device_ids[:, None] * BLK_DEV + row_pairs[:, :, 0]
    row_second = (jnp.arange(ROW_DEVS, dtype=jnp.int32)[None, :] * COL_DEVS + col_of[:, None]) * BLK_DEV + row_pairs[:, :, 1]
    col_first = device_ids[:, None] * BLK_DEV + col_pairs[:, :, 0]
    col_second = (row_of[:, None] * COL_DEVS + jnp.arange(COL_DEVS, dtype=jnp.int32)[None, :]) * BLK_DEV + col_pairs[:, :, 1]
    firsts = jnp.concatenate([row_first.reshape(-1), col_first.reshape(-1)]).astype(jnp.int32)
    seconds = jnp.concatenate([row_second.reshape(-1), col_second.reshape(-1)]).astype(jnp.int32)
    linked = jnp.concatenate([row_pairs[:, :, 0].reshape(-1) >= 0, col_pairs[:, :, 0].reshape(-1) >= 0])

    def pair_step(summed, pair_entry):
        first_block, second_block, present = pair_entry

        def include(inner):
            kernel = kernel_tile(histograms[first_block], histograms[second_block])
            inner = inner.at[first_block].add(jnp.dot(basis[second_block], kernel.T, preferred_element_type=jnp.float32))
            inner = inner.at[second_block].add(jnp.dot(basis[first_block], kernel, preferred_element_type=jnp.float32))
            return inner

        return lax.cond(present, include, lambda inner: inner, summed), None

    product, _ = lax.scan(pair_step, product, (firsts, seconds, linked))
    return product
```

```python
import jax
import jax.numpy as jnp
from jax import lax
from jax.experimental import pallas as pl
from jax.experimental.pallas import tpu as pltpu
from jax.sharding import PartitionSpec as P

F = 672
BS = 640
COLS = 32
MAIN = 640
WIDE = 768
SCALE = 1.4426950408889634 / (0.09 * F)
MESH = pl.DeviceIdType.MESH
NT = (((1,), (1,)), ((), ()))
F32 = jnp.float32
BF16 = jnp.bfloat16

OWN, X1, X2, Z1, Z2, Y1, Y2, SIB, DG = range(9)
TAB_Z, TAB_X = 9, 10
SLOTS = 9
M0, M1, SIDE, SQ, TAB, SIDE_B = range(6)

STEPS0 = [(0, 0), (0, 0), (0, 0), (0, 1), (0, 3), (1, 3), (0, 5), (7, 5), (0, 0), (7, 6), (0, 6), (1, 4), (2, 3), (0, 2), (0, 4), (0, 8)]
STEPS1 = [(0, 0), (0, 0), (0, 7), (0, 1), (0, 3), (1, 3), (0, 5), (7, 5), (0, 0), (0, 0), (0, 6), (1, 4), (2, 3), (0, 2), (0, 4), (0, 8)]
COL_STEPS = (2, 6, 7, 9, 10)
N_STEPS = 16


def pick(index, values):
    result = values[-1]
    for position in range(len(values) - 2, -1, -1):
        result = jnp.where(index == position, values[position], result)
    return result


def item_kernel(hist, basis, row_table, col_table, out, H, X, S, Q, T, QC, BR, ACC, RET, STA, STB,
                in_sem, send_sem, recv_sem, back_send, back_recv):
    r = lax.axis_index("row")
    c = lax.axis_index("col")
    z, x, y, k = r // 4, lax.rem(r, 4), c // 2, lax.rem(c, 2)
    s = 1 - 2 * k

    def row_at(dx, dz):
        return lax.rem(z + s * dz + 8, 4) * 4 + lax.rem(x + s * dx + 8, 4)

    def col_at(dy):
        return lax.rem(y + s * dy + 8, 4) * 2 + k

    def on_row(dx, dz):
        return (row_at(dx, dz), c)

    def on_col(dy):
        return (r, col_at(dy))

    sibling = (r, y * 2 + 1 - k)
    cross = (r, lax.rem(y + s + 4, 4) * 2 + 1 - k)
    sib_owner_col = jnp.where(k == 0, cross[1], sibling[1])

    peers = [on_row(1, 0), on_row(-1, 0), on_row(2, 0), on_row(0, 1), on_row(0, -1), on_row(0, 2),
             on_row(1, 1), on_row(-1, -1), on_col(1), on_col(-1), on_col(2), sibling, cross]
    barrier = pltpu.get_barrier_semaphore()
    for peer in peers:
        pl.semaphore_signal(barrier, inc=1, device_id=peer, device_id_type=MESH)

    def copies_in(b):
        return [pltpu.make_async_copy(hist.at[b], H.at[b], in_sem.at[b]),
                pltpu.make_async_copy(hist.at[b, :, pl.ds(0, MAIN)], X.at[OWN, b, :, pl.ds(0, MAIN)], in_sem.at[2 + b])]

    for b in range(2):
        for item in copies_in(b):
            item.start()

    ACC[...] = jnp.zeros_like(ACC)

    def load_table(i, carry):
        T[OWN, 2 * i] = row_table[0, i, 0]
        T[OWN, 2 * i + 1] = row_table[0, i, 1]
        return carry

    lax.fori_loop(0, 16, load_table, 0)

    def load_col(i, carry):
        T[OWN, 32 + 2 * i] = col_table[0, i, 0]
        T[OWN, 33 + 2 * i] = col_table[0, i, 1]
        return carry

    lax.fori_loop(0, 8, load_col, 0)

    lane = lax.broadcasted_iota(jnp.int32, (BS, 128), 1)
    low = lane < 32

    BR[OWN] = basis[...]
    basis_cols = jnp.concatenate([jnp.zeros((64, BS), F32), basis[0].astype(F32), basis[1].astype(F32)], axis=0).T
    for b in range(2):
        for item in copies_in(b):
            item.wait()
        X[OWN, b, :, MAIN:WIDE] = jnp.zeros((BS, 128), BF16)
        X[OWN, b, :, MAIN:F] = H[b, :, MAIN:F]
    tails = [X[OWN, b, :, MAIN:WIDE].astype(F32) for b in range(2)]
    S[OWN] = (basis_cols + tails[0] + pltpu.roll(tails[1], 32, 1)).astype(BF16)
    for b in range(2):
        values = X[OWN, b].astype(F32)
        column = jnp.sum(values * values, axis=1, keepdims=True) * (-SCALE)
        QC[OWN, b] = column
        Q[OWN, b:b + 1] = jnp.broadcast_to(column, (BS, 128)).T[0:1]

    pl.semaphore_wait(barrier, len(peers))

    def remote(src, dst, send, recv, device):
        return pltpu.make_async_remote_copy(src_ref=src, dst_ref=dst, send_sem=send, recv_sem=recv,
                                            device_id=device, device_id_type=MESH)

    def part(kind, slot):
        if kind in (M0, M1):
            return X.at[slot, kind, :, pl.ds(0, MAIN)]
        return {SIDE: S, SQ: Q, TAB: T}[kind].at[slot]

    def copy(path, kind, src, dst, device):
        return remote(part(kind, src), part(kind, dst), send_sem.at[path, kind], recv_sem.at[dst, kind], device)

    def arrived(kind, slot):
        copy(0, kind, slot, slot, sibling).wait_recv()

    paths = [(0, OWN, X1, on_row(1, 0)), (1, OWN, Z1, on_row(0, 1)), (2, OWN, Y1, on_col(1)),
             (4, X1, X2, on_row(1, 0)), (5, Z1, Z2, on_row(0, 1)), (6, Y1, Y2, on_col(1))]
    small = (TAB, SQ, SIDE)

    for kind in (TAB, SQ, SIDE, M0, M1):
        for path in paths[:3]:
            copy(path[0], kind, *path[1:]).start()
        if kind == TAB:
            copy(9, TAB, OWN, TAB_Z, on_row(0, -1)).start()
            copy(10, TAB, OWN, TAB_X, on_row(-1, 0)).start()

        @pl.when(k == 0)
        def _():
            copy(3, kind, OWN, SIB, sibling).start()

    def prepare(slot, as_left):
        side = S[slot].astype(F32)
        X[slot, 0, :, MAIN:WIDE] = jnp.where(low, side, 0.0).astype(BF16)
        X[slot, 1, :, MAIN:WIDE] = jnp.where(low, pltpu.roll(side, 96, 1), 0.0).astype(BF16)
        if as_left:
            rows = side.T
            BR[slot, 0] = rows[64:96].astype(BF16)
            BR[slot, 1] = rows[96:128].astype(BF16)
            columns = Q[slot].T
            QC[slot, 0] = columns[:, 0:1]
            QC[slot, 1] = columns[:, 1:2]

    def row_of(slot):
        return pick(slot, [r, row_at(-1, 0), row_at(-2, 0), row_at(0, -1), row_at(0, -2), r, r, r, row_at(-1, -1)])

    def col_of(slot):
        return pick(slot, [c, c, c, c, c, col_at(-1), col_at(-2), sib_owner_col, c])

    def chosen(i, j, ki, kj):
        return jnp.maximum(T[i, kj], T[j, ki + 1]), jnp.maximum(T[i, kj + 1], T[j, ki])

    def stage_a():
        target, owner = 2 * row_at(0, 1), 2 * row_at(-1, 0)
        return jnp.maximum(T[X1, target], T[TAB_Z, owner + 1])

    def stage_b():
        target, owner = 2 * row_at(1, 0), 2 * row_at(0, -1)
        return jnp.maximum(T[Z1, target], T[TAB_X, owner + 1])

    first, second = pl.ds(0, BS // 2), pl.ds(BS // 2, BS // 2)
    to_z, to_x = on_row(0, 1), on_row(1, 0)

    def diagonal_copies():
        return [
            remote(STA, X.at[DG, 0, first, pl.ds(0, MAIN)], send_sem.at[7, M0], recv_sem.at[DG, M0], to_z),
            remote(S.at[X1, first], S.at[DG, first], send_sem.at[7, SIDE], recv_sem.at[DG, SIDE], to_z),
            copy(7, SQ, X1, DG, to_z),
            copy(7, TAB, X1, DG, to_z),
            remote(STB, X.at[DG, 0, second, pl.ds(0, MAIN)], send_sem.at[8, M1], recv_sem.at[DG, M1], to_x),
            remote(S.at[Z1, second], S.at[DG, second], send_sem.at[8, SIDE], recv_sem.at[DG, SIDE_B], to_x),
        ]

    owners = [None, on_row(-1, 0), on_row(-2, 0), on_row(0, -1), on_row(0, -2), on_col(-1), on_col(-2),
              (r, sib_owner_col), on_row(-1, -1)]

    def give_back(slot):
        return remote(ACC.at[slot], RET.at[slot - 1], back_send.at[slot - 1], back_recv.at[slot - 1], owners[slot])

    def step_body(step, carry):
        @pl.when(jnp.logical_and(step == 2, k == 1))
        def _():
            for kind in (TAB, SQ, SIDE, M0, M1):
                arrived(kind, SIB)
            prepare(SIB, True)

        @pl.when(step == 3)
        def _():
            for slot in (X1, Z1, Y1):
                for kind in small:
                    arrived(kind, slot)
            arrived(TAB, TAB_Z)
            arrived(TAB, TAB_X)
            for kind in small:
                for path in paths[3:]:
                    copy(path[0], kind, *path[1:]).start()

                @pl.when(k == 1)
                def _():
                    copy(3, kind, Y1, SIB, sibling).start()
            for slot in (X1, Z1, Y1):
                prepare(slot, slot == X1)
            for kind in (M0, M1):
                for slot, path in zip((X1, Z1, Y1), paths[3:]):
                    arrived(kind, slot)
                    copy(path[0], kind, *path[1:]).start()

                @pl.when(k == 1)
                def _():
                    copy(3, kind, Y1, SIB, sibling).start()

        @pl.when(jnp.logical_and(step == 7, k == 0))
        def _():
            for kind in (TAB, SQ, SIDE, M0, M1):
                arrived(kind, SIB)
            prepare(SIB, True)

        @pl.when(step == 8)
        def _():
            STA[...] = jnp.where(stage_a() == 0, X[X1, 0, 0:BS // 2, 0:MAIN], X[X1, 1, 0:BS // 2, 0:MAIN])
            STB[...] = jnp.where(stage_b() == 0, X[Z1, 0, BS // 2:BS, 0:MAIN], X[Z1, 1, BS // 2:BS, 0:MAIN])
            for item in diagonal_copies():
                item.start()

        @pl.when(step == 9)
        def _():
            for kind in (TAB, SQ, SIDE, M0, M1):
                arrived(kind, Y2)
            prepare(Y2, False)

        @pl.when(step == 11)
        def _():
            for slot in (Y1, Y2, SIB):
                give_back(slot).start()
            for slot in (X2, Z2):
                for kind in (TAB, SQ, SIDE, M0, M1):
                    arrived(kind, slot)
                prepare(slot, slot == X2)

        @pl.when(step == 15)
        def _():
            for slot in (X1, X2, Z1, Z2):
                give_back(slot).start()
            for item in diagonal_copies():
                item.wait_recv()
            side = S[DG].astype(F32)
            own_key, their_key = 2 * r, 2 * row_at(-1, -1)
            theirs = jnp.maximum(T[OWN, their_key + 1], T[DG, own_key])
            tail = jnp.where(theirs == 0, side, pltpu.roll(side, 96, 1))
            X[DG, 0, :, MAIN:WIDE] = jnp.where(low, tail, 0.0).astype(BF16)

        i = pick(step, [jnp.where(k == 0, a[0], b[0]) if a != b else a[0] for a, b in zip(STEPS0, STEPS1)])
        j = pick(step, [jnp.where(k == 0, a[1], b[1]) if a != b else a[1] for a, b in zip(STEPS0, STEPS1)])
        west = x < 2
        i = jnp.where(jnp.logical_and(step == 13, jnp.logical_not(west)), X2, i)
        j = jnp.where(jnp.logical_and(step == 13, jnp.logical_not(west)), Z2, j)
        runs = step != 8
        runs = jnp.logical_and(runs, jnp.logical_or(step != 2, k == 1))
        runs = jnp.logical_and(runs, jnp.logical_or(step != 9, k == 0))
        runs = jnp.logical_and(runs, jnp.logical_or(step != 10, y < 2))
        runs = jnp.logical_and(runs, jnp.logical_or(step != 14, z < 2))

        @pl.when(runs)
        def _():
            along_col = step == COL_STEPS[0]
            for other in COL_STEPS[1:]:
                along_col = jnp.logical_or(along_col, step == other)
            ki = jnp.where(along_col, 32 + 2 * col_of(i), 2 * row_of(i))
            kj = jnp.where(along_col, 32 + 2 * col_of(j), 2 * row_of(j))
            bi, bj = chosen(i, j, ki, kj)
            diagonal = step < 2
            bi = jnp.where(diagonal, step, bi)
            bj = jnp.where(diagonal, step, bj)
            at = jnp.where(j == DG, 0, bj)
            left = jnp.where(bi == 0, X[i, 0], X[i, 1])
            right = jnp.where(at == 0, X[j, 0], X[j, 1])
            inner = lax.dot_general(left, right, NT, preferred_element_type=F32)
            squares = jnp.where(bi == 0, QC[i, 0], QC[i, 1]) + jnp.where(bj == 0, Q[j, 0:1], Q[j, 1:2])
            kernel = jnp.exp2(jnp.minimum(inner * (2 * SCALE) + squares, 0.0)).astype(BF16)
            theirs = jnp.dot(kernel, S[j], preferred_element_type=F32).T
            theirs = jnp.where(bj == 0, theirs[64:96], theirs[96:128])
            mine = jnp.dot(jnp.where(bi == 0, BR[i, 0], BR[i, 1]), kernel, preferred_element_type=F32)
            for b in range(2):
                ACC[i, b] += jnp.where(jnp.logical_and(bi == b, jnp.logical_not(diagonal)), theirs, 0.0)
                ACC[j, b] += jnp.where(bj == b, mine, 0.0)

        return carry

    lax.fori_loop(0, N_STEPS, step_body, 0)
    give_back(DG).start()

    for path in paths:
        for kind in (TAB, SQ, SIDE, M0, M1):
            copy(path[0], kind, *path[1:]).wait_send()
    for kind in (TAB, SQ, SIDE, M0, M1):
        copy(3, kind, OWN, SIB, sibling).wait_send()
    copy(9, TAB, OWN, TAB_Z, on_row(0, -1)).wait_send()
    copy(10, TAB, OWN, TAB_X, on_row(-1, 0)).wait_send()
    for item in diagonal_copies():
        item.wait_send()
    total = ACC[OWN]
    for slot in (Y1, Y2, SIB, X1, X2, Z1, Z2, DG):
        give_back(slot).wait()
        total = total + RET[slot - 1]
    out[...] = total


def body(histograms, basis, row_pairs, col_pairs):
    return pl.pallas_call(
        item_kernel,
        out_shape=jax.ShapeDtypeStruct((2, COLS, BS), F32),
        in_specs=[
            pl.BlockSpec(memory_space=pl.ANY),
            pl.BlockSpec(memory_space=pltpu.VMEM),
            pl.BlockSpec(memory_space=pltpu.SMEM),
            pl.BlockSpec(memory_space=pltpu.SMEM),
        ],
        out_specs=pl.BlockSpec(memory_space=pltpu.VMEM),
        scratch_shapes=[
            pltpu.VMEM((2, BS, F), BF16),
            pltpu.VMEM((SLOTS, 2, BS, WIDE), BF16),
            pltpu.VMEM((SLOTS, BS, 128), BF16),
            pltpu.VMEM((SLOTS, 8, BS), F32),
            pltpu.SMEM((11, 48), jnp.int32),
            pltpu.VMEM((SLOTS, 2, BS, 1), F32),
            pltpu.VMEM((SLOTS, 2, COLS, BS), BF16),
            pltpu.VMEM((SLOTS, 2, COLS, BS), F32),
            pltpu.VMEM((SLOTS - 1, 2, COLS, BS), F32),
            pltpu.VMEM((BS // 2, MAIN), BF16),
            pltpu.VMEM((BS // 2, MAIN), BF16),
            pltpu.SemaphoreType.DMA((4,)),
            pltpu.SemaphoreType.DMA((11, 5)),
            pltpu.SemaphoreType.DMA((11, 6)),
            pltpu.SemaphoreType.DMA((SLOTS - 1,)),
            pltpu.SemaphoreType.DMA((SLOTS - 1,)),
        ],
        compiler_params=pltpu.CompilerParams(
            collective_id=0, has_side_effects=True, vmem_limit_bytes=56 * 1024 * 1024
        ),
    )(histograms, basis, row_pairs, col_pairs)


def solution(mesh):
    spec = P(("row", "col"), None, None)
    return jax.shard_map(body, mesh=mesh, in_specs=(spec,) * 4, out_specs=spec, check_vma=False)
```

```python
import jax
import jax.numpy as jnp
from jax import lax
from jax.experimental import pallas as pl
from jax.experimental.pallas import tpu as pltpu
from jax.sharding import PartitionSpec as P

F = 672
BS = 640
COLS = 32
SCALE = 1.4426950408889634 / (0.09 * F)
MESH = pl.DeviceIdType.MESH
NT = (((1,), (1,)), ((), ()))
TN = (((0,), (0,)), ((), ()))
F32 = jnp.float32
BF16 = jnp.bfloat16

OWN, X1, X2, Z1, Z2, Y1, Y2, SIB, DG = range(9)
TAB_Z, TAB_X = 9, 10
SLOTS = 9
M0, M1, SUB, SQ, TAB = range(5)

STEPS0 = [(0, 0), (0, 0), (0, 0), (0, 1), (0, 3), (1, 3), (0, 5), (7, 5), (0, 0), (7, 6), (0, 6), (1, 4), (2, 3), (0, 2), (0, 4), (0, 8)]
STEPS1 = [(0, 0), (0, 0), (0, 7), (0, 1), (0, 3), (1, 3), (0, 5), (7, 5), (0, 0), (0, 0), (0, 6), (1, 4), (2, 3), (0, 2), (0, 4), (0, 8)]
COL_STEPS = (2, 6, 7, 9, 10)
N_STEPS = 16


def pick(index, values):
    result = values[-1]
    for position in range(len(values) - 2, -1, -1):
        result = jnp.where(index == position, values[position], result)
    return result


def item_kernel(hist, basis, row_table, col_table, out, X, B, Q, T, ACC, RET, STA, STB,
                in_sem, send_sem, recv_sem, back_send, back_recv):
    r = lax.axis_index("row")
    c = lax.axis_index("col")
    z, x, y, k = r // 4, lax.rem(r, 4), c // 2, lax.rem(c, 2)
    s = 1 - 2 * k

    def row_at(dx, dz):
        return lax.rem(z + s * dz + 8, 4) * 4 + lax.rem(x + s * dx + 8, 4)

    def col_at(dy):
        return lax.rem(y + s * dy + 8, 4) * 2 + k

    def on_row(dx, dz):
        return (row_at(dx, dz), c)

    def on_col(dy):
        return (r, col_at(dy))

    sibling = (r, y * 2 + 1 - k)
    cross = (r, lax.rem(y + s + 4, 4) * 2 + 1 - k)
    sib_owner_col = jnp.where(k == 0, cross[1], sibling[1])

    peers = [on_row(1, 0), on_row(-1, 0), on_row(2, 0), on_row(0, 1), on_row(0, -1), on_row(0, 2),
             on_row(1, 1), on_row(-1, -1), on_col(1), on_col(-1), on_col(2), sibling, cross]
    barrier = pltpu.get_barrier_semaphore()
    for peer in peers:
        pl.semaphore_signal(barrier, inc=1, device_id=peer, device_id_type=MESH)

    copies_in = [pltpu.make_async_copy(hist.at[b], X.at[OWN, b], in_sem.at[b]) for b in range(2)]
    copies_in.append(pltpu.make_async_copy(basis, B.at[OWN], in_sem.at[2]))
    for item in copies_in:
        item.start()

    ACC[...] = jnp.zeros_like(ACC)

    def load_table(i, carry):
        T[OWN, 2 * i] = row_table[0, 0, i]
        T[OWN, 2 * i + 1] = row_table[0, 1, i]
        return carry

    lax.fori_loop(0, 16, load_table, 0)

    def load_col(i, carry):
        T[OWN, 32 + 2 * i] = col_table[0, 0, i]
        T[OWN, 33 + 2 * i] = col_table[0, 1, i]
        return carry

    lax.fori_loop(0, 8, load_col, 0)

    for item in copies_in:
        item.wait()
    for b in range(2):
        values = X[OWN, b].astype(F32)
        Q[OWN, b:b + 1] = jnp.sum(values * values, axis=0, keepdims=True) * (-SCALE)

    pl.semaphore_wait(barrier, len(peers))

    def remote(src, dst, send, recv, device):
        return pltpu.make_async_remote_copy(src_ref=src, dst_ref=dst, send_sem=send, recv_sem=recv,
                                            device_id=device, device_id_type=MESH)

    def part(kind, slot):
        if kind in (M0, M1):
            return X.at[slot, kind]
        return {SUB: B, SQ: Q, TAB: T}[kind].at[slot]

    def copy(path, kind, src, dst, device):
        return remote(part(kind, src), part(kind, dst), send_sem.at[path, kind], recv_sem.at[dst, kind], device)

    def arrived(kind, slot):
        copy(0, kind, slot, slot, sibling).wait_recv()

    paths = [(0, OWN, X1, on_row(1, 0)), (1, OWN, Z1, on_row(0, 1)), (2, OWN, Y1, on_col(1)),
             (4, X1, X2, on_row(1, 0)), (5, Z1, Z2, on_row(0, 1)), (6, Y1, Y2, on_col(1))]
    small = (TAB, SQ, SUB)

    for kind in (TAB, SQ, SUB, M0, M1):
        for path in paths[:3]:
            copy(path[0], kind, *path[1:]).start()
        if kind == TAB:
            copy(9, TAB, OWN, TAB_Z, on_row(0, -1)).start()
            copy(10, TAB, OWN, TAB_X, on_row(-1, 0)).start()

        @pl.when(k == 0)
        def _():
            copy(3, kind, OWN, SIB, sibling).start()

    def row_of(slot):
        return pick(slot, [r, row_at(-1, 0), row_at(-2, 0), row_at(0, -1), row_at(0, -2), r, r, r, row_at(-1, -1)])

    def col_of(slot):
        return pick(slot, [c, c, c, c, c, col_at(-1), col_at(-2), sib_owner_col, c])

    def chosen(i, j, ki, kj):
        return jnp.maximum(T[i, kj], T[j, ki + 1]), jnp.maximum(T[i, kj + 1], T[j, ki])

    def stage_a():
        target, owner = 2 * row_at(0, 1), 2 * row_at(-1, 0)
        return jnp.maximum(T[X1, target], T[TAB_Z, owner + 1])

    def stage_b():
        target, owner = 2 * row_at(1, 0), 2 * row_at(0, -1)
        return jnp.maximum(T[Z1, target], T[TAB_X, owner + 1])

    first, second = pl.ds(0, F // 2), pl.ds(F // 2, F // 2)
    to_z, to_x = on_row(0, 1), on_row(1, 0)

    def diagonal_copies():
        return [
            copy(7, TAB, X1, DG, to_z),
            copy(7, SQ, X1, DG, to_z),
            copy(8, SUB, Z1, DG, to_x),
            remote(STA, X.at[DG, 0, first], send_sem.at[7, M0], recv_sem.at[DG, M0], to_z),
            remote(STB, X.at[DG, 0, second], send_sem.at[8, M1], recv_sem.at[DG, M1], to_x),
        ]

    owners = [None, on_row(-1, 0), on_row(-2, 0), on_row(0, -1), on_row(0, -2), on_col(-1), on_col(-2),
              (r, sib_owner_col), on_row(-1, -1)]

    def give_back(slot):
        return remote(ACC.at[slot], RET.at[slot - 1], back_send.at[slot - 1], back_recv.at[slot - 1], owners[slot])

    def step_body(step, carry):
        @pl.when(jnp.logical_and(step == 2, k == 1))
        def _():
            for kind in (TAB, SQ, SUB, M0, M1):
                arrived(kind, SIB)

        @pl.when(step == 3)
        def _():
            for slot in (X1, Z1, Y1):
                for kind in small:
                    arrived(kind, slot)
            arrived(TAB, TAB_Z)
            arrived(TAB, TAB_X)
            for kind in small:
                for path in paths[3:]:
                    copy(path[0], kind, *path[1:]).start()

                @pl.when(k == 1)
                def _():
                    copy(3, kind, Y1, SIB, sibling).start()
            for kind in (M0, M1):
                for slot, path in zip((X1, Z1, Y1), paths[3:]):
                    arrived(kind, slot)
                    copy(path[0], kind, *path[1:]).start()

                @pl.when(k == 1)
                def _():
                    copy(3, kind, Y1, SIB, sibling).start()

        @pl.when(jnp.logical_and(step == 7, k == 0))
        def _():
            for kind in (TAB, SQ, SUB, M0, M1):
                arrived(kind, SIB)

        @pl.when(step == 8)
        def _():
            STA[...] = jnp.where(stage_a() == 0, X[X1, 0, 0:F // 2], X[X1, 1, 0:F // 2])
            STB[...] = jnp.where(stage_b() == 0, X[Z1, 0, F // 2:F], X[Z1, 1, F // 2:F])
            for item in diagonal_copies():
                item.start()

        @pl.when(step == 9)
        def _():
            for kind in (TAB, SQ, SUB, M0, M1):
                arrived(kind, Y2)

        @pl.when(step == 11)
        def _():
            for slot in (Y1, Y2, SIB):
                give_back(slot).start()
            for slot in (X2, Z2):
                for kind in (TAB, SQ, SUB, M0, M1):
                    arrived(kind, slot)

        @pl.when(step == 15)
        def _():
            for slot in (X1, X2, Z1, Z2):
                give_back(slot).start()
            for item in diagonal_copies():
                item.wait_recv()

        i = pick(step, [jnp.where(k == 0, a[0], b[0]) if a != b else a[0] for a, b in zip(STEPS0, STEPS1)])
        j = pick(step, [jnp.where(k == 0, a[1], b[1]) if a != b else a[1] for a, b in zip(STEPS0, STEPS1)])
        west = x < 2
        i = jnp.where(jnp.logical_and(step == 13, jnp.logical_not(west)), X2, i)
        j = jnp.where(jnp.logical_and(step == 13, jnp.logical_not(west)), Z2, j)
        runs = step != 8
        runs = jnp.logical_and(runs, jnp.logical_or(step != 2, k == 1))
        runs = jnp.logical_and(runs, jnp.logical_or(step != 9, k == 0))
        runs = jnp.logical_and(runs, jnp.logical_or(step != 10, y < 2))
        runs = jnp.logical_and(runs, jnp.logical_or(step != 14, z < 2))

        @pl.when(runs)
        def _():
            along_col = step == COL_STEPS[0]
            for other in COL_STEPS[1:]:
                along_col = jnp.logical_or(along_col, step == other)
            ki = jnp.where(along_col, 32 + 2 * col_of(i), 2 * row_of(i))
            kj = jnp.where(along_col, 32 + 2 * col_of(j), 2 * row_of(j))
            bi, bj = chosen(i, j, ki, kj)
            diagonal = step < 2
            bi = jnp.where(diagonal, step, bi)
            bj = jnp.where(diagonal, step, bj)
            at = jnp.where(j == DG, 0, bj)
            left = jnp.where(bi == 0, X[i, 0], X[i, 1])
            right = jnp.where(at == 0, X[j, 0], X[j, 1])
            inner = lax.dot_general(left, right, TN, preferred_element_type=F32)
            left_squares = jnp.where(bi == 0, Q[i, 0:1], Q[i, 1:2])
            right_squares = jnp.where(bj == 0, Q[j, 0:1], Q[j, 1:2])
            squares = jnp.broadcast_to(left_squares, (8, BS)).T[:, 0:1] + right_squares
            kernel = jnp.exp2(jnp.minimum(inner * (2 * SCALE) + squares, 0.0)).astype(BF16)
            left_basis = jnp.where(bi == 0, B[i, 0], B[i, 1])
            right_basis = jnp.where(bj == 0, B[j, 0], B[j, 1])
            theirs = lax.dot_general(kernel, right_basis, NT, preferred_element_type=F32).T
            mine = jnp.dot(left_basis, kernel, preferred_element_type=F32)
            for b in range(2):
                ACC[i, b] += jnp.where(jnp.logical_and(bi == b, jnp.logical_not(diagonal)), theirs, 0.0)
                ACC[j, b] += jnp.where(bj == b, mine, 0.0)

        return carry

    lax.fori_loop(0, N_STEPS, step_body, 0)
    give_back(DG).start()

    for path in paths:
        for kind in (TAB, SQ, SUB, M0, M1):
            copy(path[0], kind, *path[1:]).wait_send()
    for kind in (TAB, SQ, SUB, M0, M1):
        copy(3, kind, OWN, SIB, sibling).wait_send()
    copy(9, TAB, OWN, TAB_Z, on_row(0, -1)).wait_send()
    copy(10, TAB, OWN, TAB_X, on_row(-1, 0)).wait_send()
    for item in diagonal_copies():
        item.wait_send()
    total = ACC[OWN]
    for slot in (Y1, Y2, SIB, X1, X2, Z1, Z2, DG):
        give_back(slot).wait()
        total = total + RET[slot - 1]
    out[...] = total


def body(histograms, basis, row_pairs, col_pairs):
    return pl.pallas_call(
        item_kernel,
        out_shape=jax.ShapeDtypeStruct((2, COLS, BS), F32),
        in_specs=[
            pl.BlockSpec(memory_space=pl.ANY),
            pl.BlockSpec(memory_space=pl.ANY),
            pl.BlockSpec(memory_space=pltpu.SMEM),
            pl.BlockSpec(memory_space=pltpu.SMEM),
        ],
        out_specs=pl.BlockSpec(memory_space=pltpu.VMEM),
        scratch_shapes=[
            pltpu.VMEM((SLOTS, 2, F, BS), BF16),
            pltpu.VMEM((SLOTS, 2, COLS, BS), BF16),
            pltpu.VMEM((SLOTS, 8, BS), F32),
            pltpu.SMEM((11, 48), jnp.int32),
            pltpu.VMEM((SLOTS, 2, COLS, BS), F32),
            pltpu.VMEM((SLOTS - 1, 2, COLS, BS), F32),
            pltpu.VMEM((F // 2, BS), BF16),
            pltpu.VMEM((F // 2, BS), BF16),
            pltpu.SemaphoreType.DMA((3,)),
            pltpu.SemaphoreType.DMA((11, 5)),
            pltpu.SemaphoreType.DMA((11, 5)),
            pltpu.SemaphoreType.DMA((SLOTS - 1,)),
            pltpu.SemaphoreType.DMA((SLOTS - 1,)),
        ],
        compiler_params=pltpu.CompilerParams(
            collective_id=0, has_side_effects=True, vmem_limit_bytes=56 * 1024 * 1024
        ),
    )(jnp.swapaxes(histograms, 1, 2), basis, jnp.swapaxes(row_pairs, 1, 2), jnp.swapaxes(col_pairs, 1, 2))


def solution(mesh):
    spec = P(("row", "col"), None, None)
    return jax.shard_map(body, mesh=mesh, in_specs=(spec,) * 4, out_specs=spec, check_vma=False)
```

```python
import jax
import jax.numpy as jnp
from jax import lax
from jax.experimental import pallas as pl
from jax.experimental.pallas import tpu as pltpu
from jax.sharding import PartitionSpec as P

F = 672
BS = 640
COLS = 32
SCALE = 1.4426950408889634 / (0.09 * F)
MESH = pl.DeviceIdType.MESH
NT = (((1,), (1,)), ((), ()))
TN = (((0,), (0,)), ((), ()))
F32 = jnp.float32
BF16 = jnp.bfloat16

OWN, X1, X2, Z1, Z2, Y1, Y2, SIB, DG = range(9)
TAB_Z, TAB_X, TAB_D = 9, 10, 11
SLOTS = 9
M0, M1, SUB, SQ, TAB = range(5)

STEPS0 = [(0, 0), (0, 0), (0, 0), (0, 1), (0, 3), (1, 3), (0, 5), (7, 5), (0, 0), (7, 6), (0, 6), (1, 4), (2, 3), (0, 2), (0, 4), (0, 8)]
STEPS1 = [(0, 0), (0, 0), (0, 7), (0, 1), (0, 3), (1, 3), (0, 5), (7, 5), (0, 0), (0, 0), (0, 6), (1, 4), (2, 3), (0, 2), (0, 4), (0, 8)]
COL_STEPS = (2, 6, 7, 9, 10)
N_STEPS = 16


def pick(index, values):
    result = values[-1]
    for position in range(len(values) - 2, -1, -1):
        result = jnp.where(index == position, values[position], result)
    return result


def item_kernel(hist, basis, row_table, col_table, out, X, B, Q, T, ACC, BACK, RET, STA, STB,
                in_sem, send_sem, recv_sem, back_send, back_recv):
    r = lax.axis_index("row")
    c = lax.axis_index("col")
    z, x, y, k = r // 4, lax.rem(r, 4), c // 2, lax.rem(c, 2)
    s = 1 - 2 * k

    def row_at(dx, dz):
        return lax.rem(z + s * dz + 8, 4) * 4 + lax.rem(x + s * dx + 8, 4)

    def col_at(dy):
        return lax.rem(y + s * dy + 8, 4) * 2 + k

    def on_row(dx, dz):
        return (row_at(dx, dz), c)

    def on_col(dy):
        return (r, col_at(dy))

    sibling = (r, y * 2 + 1 - k)
    cross = (r, lax.rem(y + s + 4, 4) * 2 + 1 - k)
    sib_owner_col = jnp.where(k == 0, cross[1], sibling[1])

    barrier = pltpu.get_barrier_semaphore()
    sources = [on_row(-1, 0), on_row(0, -1), on_col(-1), sibling]
    for source in sources:
        pl.semaphore_signal(barrier, inc=1, device_id=source, device_id_type=MESH)

    copies_in = [pltpu.make_async_copy(hist.at[b], X.at[OWN, b], in_sem.at[b]) for b in range(2)]
    copies_in.append(pltpu.make_async_copy(basis, B.at[OWN], in_sem.at[2]))
    for item in copies_in:
        item.start()

    ACC[...] = jnp.zeros_like(ACC)

    def load_table(i, carry):
        T[OWN, 2 * i] = row_table[0, 0, i]
        T[OWN, 2 * i + 1] = row_table[0, 1, i]
        return carry

    lax.fori_loop(0, 16, load_table, 0)

    def load_col(i, carry):
        T[OWN, 32 + 2 * i] = col_table[0, 0, i]
        T[OWN, 33 + 2 * i] = col_table[0, 1, i]
        return carry

    lax.fori_loop(0, 8, load_col, 0)

    for item in copies_in:
        item.wait()
    for b in range(2):
        values = X[OWN, b].astype(F32)
        Q[OWN, b:b + 1] = jnp.sum(values * values, axis=0, keepdims=True) * (-SCALE)

    pl.semaphore_wait(barrier, len(sources))

    def remote(src, dst, send, recv, device):
        return pltpu.make_async_remote_copy(src_ref=src, dst_ref=dst, send_sem=send, recv_sem=recv,
                                            device_id=device, device_id_type=MESH)

    def part(kind, slot):
        if kind in (M0, M1):
            return X.at[slot, kind]
        return {SUB: B, SQ: Q, TAB: T}[kind].at[slot]

    def copy(path, kind, src, dst, device):
        return remote(part(kind, src), part(kind, dst), send_sem.at[path, kind], recv_sem.at[dst, kind], device)

    def arrived(kind, slot):
        copy(0, kind, slot, slot, sibling).wait_recv()

    paths = [(0, OWN, X1, on_row(1, 0)), (1, OWN, Z1, on_row(0, 1)), (2, OWN, Y1, on_col(1)),
             (4, X1, X2, on_row(1, 0)), (5, Z1, Z2, on_row(0, 1)), (6, Y1, Y2, on_col(1))]
    small = (TAB, SQ, SUB)

    for kind in (TAB, SQ, SUB, M0, M1):
        for path in paths[:3]:
            copy(path[0], kind, *path[1:]).start()

        @pl.when(k == 0)
        def _():
            copy(3, kind, OWN, SIB, sibling).start()

    def row_of(slot):
        return pick(slot, [r, row_at(-1, 0), row_at(-2, 0), row_at(0, -1), row_at(0, -2), r, r, r, row_at(-1, -1)])

    def col_of(slot):
        return pick(slot, [c, c, c, c, c, col_at(-1), col_at(-2), sib_owner_col, c])

    def chosen(i, j, ki, kj):
        return jnp.maximum(T[i, kj], T[j, ki + 1]), jnp.maximum(T[i, kj + 1], T[j, ki])

    def stage_a():
        target, owner = 2 * row_at(0, 1), 2 * row_at(-1, 0)
        return jnp.maximum(T[X1, target], T[TAB_Z, owner + 1])

    def stage_b():
        target, owner = 2 * row_at(1, 0), 2 * row_at(0, -1)
        return jnp.maximum(T[Z1, target], T[TAB_X, owner + 1])

    first, second = pl.ds(0, F // 2), pl.ds(F // 2, F // 2)
    to_z, to_x = on_row(0, 1), on_row(1, 0)

    def diagonal_copies():
        return [
            copy(7, TAB, X1, DG, to_z),
            copy(7, SQ, X1, DG, to_z),
            copy(8, SUB, Z1, DG, to_x),
            remote(STA, X.at[DG, 0, first], send_sem.at[7, M0], recv_sem.at[DG, M0], to_z),
            remote(STB, X.at[DG, 0, second], send_sem.at[8, M1], recv_sem.at[DG, M1], to_x),
        ]

    owners = [None, on_row(-1, 0), on_row(-2, 0), on_row(0, -1), on_row(0, -2), on_col(-1), on_col(-2),
              (r, sib_owner_col), on_row(-1, -1)]

    def give_back(slot):
        part = (slot - 1, 0) if slot == DG else slot - 1
        return remote(BACK.at[part], RET.at[part], back_send.at[slot - 1], back_recv.at[slot - 1], owners[slot])

    def table_back():
        return remote(T.at[OWN], T.at[TAB_D], send_sem.at[7, M1], recv_sem.at[TAB_D, TAB], owners[DG])

    def start_back(slot):
        if slot == DG:
            BACK[slot - 1, 0] = (ACC[slot, 0] + ACC[slot, 1]).astype(BF16)
        else:
            BACK[slot - 1] = ACC[slot].astype(BF16)
        give_back(slot).start()

    def step_body(step, carry):
        @pl.when(jnp.logical_and(step == 2, k == 1))
        def _():
            for kind in (TAB, SQ, SUB, M0, M1):
                arrived(kind, SIB)

        @pl.when(step == 3)
        def _():
            for slot in (X1, Z1, Y1):
                for kind in small:
                    arrived(kind, slot)
            copy(9, TAB, OWN, TAB_Z, on_row(0, -1)).start()
            copy(10, TAB, OWN, TAB_X, on_row(-1, 0)).start()
            for kind in small:
                for path in paths[3:]:
                    copy(path[0], kind, *path[1:]).start()

                @pl.when(k == 1)
                def _():
                    copy(3, kind, Y1, SIB, sibling).start()
            for kind in (M0, M1):
                for slot, path in zip((X1, Z1, Y1), paths[3:]):
                    arrived(kind, slot)
                    copy(path[0], kind, *path[1:]).start()

                @pl.when(k == 1)
                def _():
                    copy(3, kind, Y1, SIB, sibling).start()

        @pl.when(jnp.logical_and(step == 7, k == 0))
        def _():
            for kind in (TAB, SQ, SUB, M0, M1):
                arrived(kind, SIB)

        @pl.when(step == 8)
        def _():
            arrived(TAB, TAB_Z)
            arrived(TAB, TAB_X)
            STA[...] = jnp.where(stage_a() == 0, X[X1, 0, 0:F // 2], X[X1, 1, 0:F // 2])
            STB[...] = jnp.where(stage_b() == 0, X[Z1, 0, F // 2:F], X[Z1, 1, F // 2:F])
            for path in paths[3:5]:
                for kind in (M0, M1):
                    copy(path[0], kind, *path[1:]).wait_send()
            for item in diagonal_copies():
                item.start()

        @pl.when(step == 9)
        def _():
            for kind in (TAB, SQ, SUB, M0, M1):
                arrived(kind, Y2)

        @pl.when(step == 11)
        def _():
            for slot in (Y1, Y2, SIB):
                start_back(slot)
            for slot in (X2, Z2):
                for kind in (TAB, SQ, SUB, M0, M1):
                    arrived(kind, slot)

        for ready, slot in ((12, X1), (13, Z1), (14, X2)):
            @pl.when(step == ready)
            def _():
                start_back(slot)

        @pl.when(step == 15)
        def _():
            start_back(Z2)
            for item in diagonal_copies():
                item.wait_recv()
            table_back().start()

        i = pick(step, [jnp.where(k == 0, a[0], b[0]) if a != b else a[0] for a, b in zip(STEPS0, STEPS1)])
        j = pick(step, [jnp.where(k == 0, a[1], b[1]) if a != b else a[1] for a, b in zip(STEPS0, STEPS1)])
        west = x < 2
        i = jnp.where(jnp.logical_and(step == 13, jnp.logical_not(west)), X2, i)
        j = jnp.where(jnp.logical_and(step == 13, jnp.logical_not(west)), Z2, j)
        runs = step != 8
        runs = jnp.logical_and(runs, jnp.logical_or(step != 2, k == 1))
        runs = jnp.logical_and(runs, jnp.logical_or(step != 9, k == 0))
        runs = jnp.logical_and(runs, jnp.logical_or(step != 10, y < 2))
        runs = jnp.logical_and(runs, jnp.logical_or(step != 14, z < 2))

        @pl.when(runs)
        def _():
            along_col = step == COL_STEPS[0]
            for other in COL_STEPS[1:]:
                along_col = jnp.logical_or(along_col, step == other)
            ki = jnp.where(along_col, 32 + 2 * col_of(i), 2 * row_of(i))
            kj = jnp.where(along_col, 32 + 2 * col_of(j), 2 * row_of(j))
            bi, bj = chosen(i, j, ki, kj)
            diagonal = step < 2
            bi = jnp.where(diagonal, step, bi)
            bj = jnp.where(diagonal, step, bj)
            at = jnp.where(j == DG, 0, bj)
            left = jnp.where(bi == 0, X[i, 0], X[i, 1])
            right = jnp.where(at == 0, X[j, 0], X[j, 1])
            inner = lax.dot_general(left, right, TN, preferred_element_type=F32)
            left_squares = jnp.where(bi == 0, Q[i, 0:1], Q[i, 1:2])
            right_squares = jnp.where(bj == 0, Q[j, 0:1], Q[j, 1:2])
            squares = jnp.broadcast_to(left_squares, (8, BS)).T[:, 0:1] + right_squares
            kernel = jnp.exp2(jnp.minimum(inner * (2 * SCALE) + squares, 0.0)).astype(BF16)
            left_basis = jnp.where(bi == 0, B[i, 0], B[i, 1])
            right_basis = jnp.where(bj == 0, B[j, 0], B[j, 1])
            theirs = lax.dot_general(kernel, right_basis, NT, preferred_element_type=F32).T
            mine = jnp.dot(left_basis, kernel, preferred_element_type=F32)
            for b in range(2):
                ACC[i, b] += jnp.where(jnp.logical_and(bi == b, jnp.logical_not(diagonal)), theirs, 0.0)
                ACC[j, b] += jnp.where(bj == b, mine, 0.0)

        return carry

    lax.fori_loop(0, N_STEPS, step_body, 0)
    start_back(DG)
    total = [ACC[OWN, b] for b in range(2)]
    for slot in (Y1, Y2, SIB, X1, Z1, X2, Z2):
        give_back(slot).wait()
        for b in range(2):
            total[b] = total[b] + RET[slot - 1, b].astype(F32)
    for path in paths:
        for kind in (TAB, SQ, SUB, M0, M1):
            if kind not in (M0, M1) or path not in paths[3:5]:
                copy(path[0], kind, *path[1:]).wait_send()
    for kind in (TAB, SQ, SUB, M0, M1):
        copy(3, kind, OWN, SIB, sibling).wait_send()
    copy(9, TAB, OWN, TAB_Z, on_row(0, -1)).wait_send()
    copy(10, TAB, OWN, TAB_X, on_row(-1, 0)).wait_send()
    for item in diagonal_copies():
        item.wait_send()
    table_back().wait()
    mine = jnp.maximum(T[OWN, 2 * row_at(1, 1)], T[TAB_D, 2 * r + 1])
    give_back(DG).wait()
    last = RET[DG - 1, 0].astype(F32)
    for b in range(2):
        out[b] = total[b] + jnp.where(mine == b, last, 0.0)


def body(histograms, basis, row_pairs, col_pairs):
    return pl.pallas_call(
        item_kernel,
        out_shape=jax.ShapeDtypeStruct((2, COLS, BS), F32),
        in_specs=[
            pl.BlockSpec(memory_space=pl.ANY),
            pl.BlockSpec(memory_space=pl.ANY),
            pl.BlockSpec(memory_space=pltpu.SMEM),
            pl.BlockSpec(memory_space=pltpu.SMEM),
        ],
        out_specs=pl.BlockSpec(memory_space=pltpu.VMEM),
        scratch_shapes=[
            pltpu.VMEM((SLOTS, 2, F, BS), BF16),
            pltpu.VMEM((SLOTS, 2, COLS, BS), BF16),
            pltpu.VMEM((SLOTS, 8, BS), F32),
            pltpu.SMEM((12, 48), jnp.int32),
            pltpu.VMEM((SLOTS, 2, COLS, BS), F32),
            pltpu.VMEM((SLOTS - 1, 2, COLS, BS), BF16),
            pltpu.VMEM((SLOTS - 1, 2, COLS, BS), BF16),
            pltpu.VMEM((F // 2, BS), BF16),
            pltpu.VMEM((F // 2, BS), BF16),
            pltpu.SemaphoreType.DMA((3,)),
            pltpu.SemaphoreType.DMA((12, 5)),
            pltpu.SemaphoreType.DMA((12, 5)),
            pltpu.SemaphoreType.DMA((SLOTS - 1,)),
            pltpu.SemaphoreType.DMA((SLOTS - 1,)),
        ],
        compiler_params=pltpu.CompilerParams(
            collective_id=0, has_side_effects=True, vmem_limit_bytes=56 * 1024 * 1024
        ),
    )(jnp.swapaxes(histograms, 1, 2), basis, jnp.swapaxes(row_pairs, 1, 2), jnp.swapaxes(col_pairs, 1, 2))


def solution(mesh):
    spec = P(("row", "col"), None, None)
    return jax.shard_map(body, mesh=mesh, in_specs=(spec,) * 4, out_specs=spec, check_vma=False)
```

```python
import jax
import jax.numpy as jnp
from jax import lax
from jax.experimental import pallas as pl
from jax.experimental.pallas import tpu as pltpu
from jax.sharding import PartitionSpec as P

F = 672
BS = 640
COLS = 32
SCALE = 1.4426950408889634 / (0.09 * F)
MESH = pl.DeviceIdType.MESH
NT = (((1,), (1,)), ((), ()))
TN = (((0,), (0,)), ((), ()))
F32 = jnp.float32
BF16 = jnp.bfloat16

OWN, X1, X2, Z1, Z2, Y1, Y2, SIB, DG, YN = range(10)
TAB_Z, TAB_X, TAB_D, TAB_Y, TAB_S = range(10, 15)
SLOTS = 10
M0, M1, N0, N1, SUB, SQ, TAB = range(7)
BULK, SMALL = (M0, M1, N0, N1), (TAB, SQ, SUB)
CUT = 512

STEPS = [
    ((0, 0), (0, 0)),
    ((0, 1), (0, 3)),
    ((1, 3), (0, 5)),
    ((7, 5), (0, 7)),
    ((0, 6), (0, 0)),
]
COL_PAIRS = ((2, 1), (3, 0), (3, 1), (4, 0))
LAST_STEPS = [
    ((1, 4), (2, 3)),
    ((0, 2), (0, 4)),
]


def pick(index, values):
    result = values[-1]
    for position in range(len(values) - 2, -1, -1):
        result = jnp.where(index == position, values[position], result)
    return result


def item_kernel(hist, basis, row_table, col_table, out, X, B, Q, T, ACC, BACK, RET, STA, STB, STC, G,
                in_sem, send_sem, recv_sem, back_send, back_recv):
    r = lax.axis_index("row")
    c = lax.axis_index("col")
    z, x, y, k = r // 4, lax.rem(r, 4), c // 2, lax.rem(c, 2)
    s = 1 - 2 * k

    def row_at(dx, dz):
        return lax.rem(z + s * dz + 8, 4) * 4 + lax.rem(x + s * dx + 8, 4)

    def col_at(dy):
        return lax.rem(y + s * dy + 8, 4) * 2 + k

    def on_row(dx, dz):
        return (row_at(dx, dz), c)

    def on_col(dy):
        return (r, col_at(dy))

    sibling = (r, y * 2 + 1 - k)
    cross = (r, lax.rem(y + s + 4, 4) * 2 + 1 - k)
    sib_next_col = lax.rem(y + 2, 4) * 2 + 1 - k
    sib_owner_col = jnp.where(k == 0, cross[1], sibling[1])

    barrier = pltpu.get_barrier_semaphore()
    sources = [on_row(-1, 0), on_row(0, -1), on_col(-1), sibling]
    for source in sources:
        pl.semaphore_signal(barrier, inc=1, device_id=source, device_id_type=MESH)

    copies_in = [pltpu.make_async_copy(hist.at[b], X.at[OWN, b], in_sem.at[b]) for b in range(2)]
    copies_in.append(pltpu.make_async_copy(basis, B.at[OWN], in_sem.at[2]))
    for item in copies_in:
        item.start()

    ACC[...] = jnp.zeros_like(ACC)

    def load_table(i, carry):
        T[OWN, 2 * i] = row_table[0, 0, i]
        T[OWN, 2 * i + 1] = row_table[0, 1, i]
        return carry

    lax.fori_loop(0, 16, load_table, 0)

    def load_col(i, carry):
        T[OWN, 32 + 2 * i] = col_table[0, 0, i]
        T[OWN, 33 + 2 * i] = col_table[0, 1, i]
        return carry

    lax.fori_loop(0, 8, load_col, 0)

    for item in copies_in:
        item.wait()
    for b in range(2):
        values = X[OWN, b].astype(F32)
        Q[OWN, b:b + 1] = jnp.sum(values * values, axis=0, keepdims=True) * (-SCALE)

    pl.semaphore_wait(barrier, len(sources))

    def remote(src, dst, send, recv, device):
        return pltpu.make_async_remote_copy(src_ref=src, dst_ref=dst, send_sem=send, recv_sem=recv,
                                            device_id=device, device_id_type=MESH)

    def part(kind, slot):
        if kind in BULK:
            return X.at[slot, kind % 2, pl.ds(0, CUT) if kind < 2 else pl.ds(CUT, F - CUT)]
        return {SUB: B, SQ: Q, TAB: T}[kind].at[slot]

    def copy(path, kind, src, dst, device):
        return remote(part(kind, src), part(kind, dst), send_sem.at[path, kind], recv_sem.at[dst, kind], device)

    def arrived(kind, slot):
        copy(0, kind, slot, slot, sibling).wait_recv()

    paths = [(0, OWN, X1, on_row(1, 0)), (1, OWN, Z1, on_row(0, 1)), (2, OWN, Y1, on_col(1)),
             (4, X1, X2, on_row(1, 0)), (5, Z1, Z2, on_row(0, 1)), (6, Y1, Y2, on_col(1))]

    def send_own(kind):
        for path in paths[:3]:
            copy(path[0], kind, *path[1:]).start()

        @pl.when(k == 0)
        def _():
            copy(3, kind, OWN, SIB, sibling).start()

    for kind in SMALL + (M0,):
        send_own(kind)

    def row_of(slot):
        return pick(slot, [r, row_at(-1, 0), row_at(-2, 0), row_at(0, -1), row_at(0, -2), r, r, r, row_at(-1, -1), r])

    def col_of(slot):
        return pick(slot, [c, c, c, c, c, col_at(-1), col_at(-2), sib_owner_col, c, col_at(1)])

    def chosen(i, j, ki, kj):
        return jnp.maximum(T[i, kj], T[j, ki + 1]), jnp.maximum(T[i, kj + 1], T[j, ki])

    def stage_a():
        target, owner = 2 * row_at(0, 1), 2 * row_at(-1, 0)
        return jnp.maximum(T[X1, target], T[TAB_Z, owner + 1])

    def stage_b():
        target, owner = 2 * row_at(1, 0), 2 * row_at(0, -1)
        return jnp.maximum(T[Z1, target], T[TAB_X, owner + 1])

    def stage_cross():
        return jnp.maximum(T[Y1, 32 + 2 * sib_next_col], T[TAB_S, 33 + 2 * col_at(-1)])

    def stage_far():
        return jnp.maximum(T[Y1, 32 + 2 * col_at(1)], T[TAB_Y, 33 + 2 * col_at(-1)])

    def stage_back():
        return jnp.maximum(T[OWN, 32 + 2 * col_at(-2)], T[Y2, 33 + 2 * c])

    def second_y():
        return remote(STC.at[0], X.at[Y2, 0], send_sem.at[6, M0], recv_sem.at[Y2, M0], on_col(1))

    def next_y():
        return [copy(13, kind, OWN, YN, on_col(-1)) for kind in SMALL] + [
            remote(STC.at[1], X.at[YN, 0], send_sem.at[13, M0], recv_sem.at[YN, M0], on_col(-1))]

    def sibling_table():
        return remote(T.at[Y2], T.at[TAB_S], send_sem.at[12, TAB], recv_sem.at[TAB_S, TAB], sibling)

    first, second = pl.ds(0, F // 2), pl.ds(F // 2, F // 2)
    to_z, to_x = on_row(0, 1), on_row(1, 0)

    def diagonal_copies():
        return [
            copy(7, TAB, X1, DG, to_z),
            copy(7, SQ, X1, DG, to_z),
            copy(8, SUB, Z1, DG, to_x),
            remote(STA, X.at[DG, 0, first], send_sem.at[7, M0], recv_sem.at[DG, M0], to_z),
            remote(STB, X.at[DG, 0, second], send_sem.at[8, M1], recv_sem.at[DG, M1], to_x),
        ]

    owners = [None, on_row(-1, 0), on_row(-2, 0), on_row(0, -1), on_row(0, -2), on_col(-1), on_col(-2),
              (r, sib_owner_col), on_row(-1, -1), on_col(1)]

    def give_back(slot):
        part = (slot - 1, 0) if slot == DG else slot - 1
        return remote(BACK.at[part], RET.at[part], back_send.at[slot - 1], back_recv.at[slot - 1], owners[slot])

    def table_back():
        return remote(T.at[OWN], T.at[TAB_D], send_sem.at[7, M1], recv_sem.at[TAB_D, TAB], owners[DG])

    def start_back(slot):
        BACK[slot - 1] = ACC[slot].astype(BF16)
        give_back(slot).start()

    west = x < 2

    def takes(dy):
        return ((z < 2) == (lax.rem(y + s * dy + 4, 4) < 2)) == (k == 1)

    takes_y, next_takes, last_takes = takes(0), takes(1), takes(-1)

    def pair_of(step, place):
        i, j = [pick(step, [entry[place][side] for entry in STEPS]) for side in range(2)]
        along_col = step < 0
        for s_col, p_col in COL_PAIRS:
            if p_col == place:
                along_col = jnp.logical_or(along_col, step == s_col)
        if place == 0:
            swap = jnp.logical_and(step == 4, k == 0)
            i, j = jnp.where(swap, Y1, i), jnp.where(swap, YN, j)
        else:
            swap = jnp.logical_and(step == 3, k == 0)
            i, j = jnp.where(swap, SIB, i), jnp.where(swap, Y2, j)
        ki = jnp.where(along_col, 32 + 2 * col_of(i), 2 * row_of(i))
        kj = jnp.where(along_col, 32 + 2 * col_of(j), 2 * row_of(j))
        bi, bj = chosen(i, j, ki, kj)
        diagonal = step == 0
        bi, bj = jnp.where(diagonal, place, bi), jnp.where(diagonal, place, bj)
        if place == 1:
            bi, bj = jnp.where(step == 4, -1, bi), jnp.where(step == 4, -1, bj)
        at = jnp.where(jnp.logical_or(j == Y2, j == YN), 0, bj)
        return i, j, bi, bj, at

    def last_pair_of(step, place):
        i, j = [pick(step, [entry[place][side] for entry in LAST_STEPS]) for side in range(2)]
        if place == 0:
            swap = jnp.logical_and(step == 1, jnp.logical_not(west))
            i, j = jnp.where(swap, X2, i), jnp.where(swap, Z2, j)
        bi, bj = chosen(i, j, 2 * row_of(i), 2 * row_of(j))
        if place == 1:
            left_out = jnp.logical_and(step == 1, takes_y)
            bi, bj = jnp.where(left_out, -1, bi), jnp.where(left_out, -1, bj)
        return i, j, bi, bj, bj

    def inner_of(i, j, bi, at, rows):
        left = jnp.where(bi == 0, X[i, 0, rows], X[i, 1, rows])
        right = X[j, at, rows] if isinstance(at, int) else jnp.where(at == 0, X[j, 0, rows], X[j, 1, rows])
        return lax.dot_general(left, right, TN, preferred_element_type=F32)

    def kernel_of(inner, i, j, bi, bj):
        left_squares = jnp.where(bi == 0, Q[i, 0:1], Q[i, 1:2])
        right_squares = jnp.where(bj == 0, Q[j, 0:1], Q[j, 1:2])
        squares = jnp.broadcast_to(left_squares, (8, BS)).T[:, 0:1] + right_squares
        return jnp.exp2(jnp.minimum(inner * (2 * SCALE) + squares, 0.0)).astype(BF16)

    def tile(i, j, bi, bj, at):
        return kernel_of(inner_of(i, j, bi, at, slice(None)), i, j, bi, bj)

    def add_terms(pairs, kernels, diagonal):
        for (i, j, bi, bj, _), kernel in zip(pairs, kernels):
            for_left, for_right = left_part(kernel, j, bj), right_part(kernel, i, bi)
            for b in range(2):
                ACC[i, b] += jnp.where(jnp.logical_and(bi == b, jnp.logical_not(diagonal)), for_left, 0.0)
                ACC[j, b] += jnp.where(bj == b, for_right, 0.0)

    def left_part(kernel, j, bj):
        right_basis = jnp.where(bj == 0, B[j, 0], B[j, 1])
        return lax.dot_general(kernel, right_basis, NT, preferred_element_type=F32).T

    def right_part(kernel, i, bi):
        return jnp.dot(jnp.where(bi == 0, B[i, 0], B[i, 1]), kernel, preferred_element_type=F32)

    def step_body(step, carry):
        @pl.when(step == 1)
        def _():
            for slot in (X1, Z1, Y1):
                for kind in SMALL:
                    arrived(kind, slot)
            copy(9, TAB, OWN, TAB_Z, on_row(0, -1)).start()
            copy(10, TAB, OWN, TAB_X, on_row(-1, 0)).start()
            copy(11, TAB, OWN, TAB_Y, on_col(-1)).start()
            for kind in SMALL:
                for path in paths[3:]:
                    copy(path[0], kind, *path[1:]).start()

                @pl.when(k == 1)
                def _():
                    copy(3, kind, Y1, SIB, sibling).start()

            for kind in BULK[1:]:
                send_own(kind)

            @pl.when(k == 1)
            def _():
                arrived(TAB, Y2)
                sibling_table().start()

            for kind in BULK:
                for slot, path in zip((X1, Z1), paths[3:]):
                    arrived(kind, slot)
                    copy(path[0], kind, *path[1:]).start()
                arrived(kind, Y1)

                @pl.when(k == 1)
                def _():
                    copy(3, kind, Y1, SIB, sibling).start()
            arrived(TAB, TAB_Y)

            @pl.when(k == 0)
            def _():
                arrived(TAB, TAB_S)
                STC[0] = jnp.where(stage_cross() == 0, X[Y1, 0], X[Y1, 1])
                second_y().start()

            @pl.when(k == 0)
            def _():
                arrived(TAB, Y2)

            @pl.when(jnp.logical_and(k == 0, last_takes))
            def _():
                STC[1] = jnp.where(stage_back() == 0, X[OWN, 0], X[OWN, 1])
                for item in next_y():
                    item.start()

            @pl.when(jnp.logical_and(k == 1, next_takes))
            def _():
                STC[0] = jnp.where(stage_far() == 0, X[Y1, 0], X[Y1, 1])
                second_y().start()

            arrived(TAB, TAB_Z)
            arrived(TAB, TAB_X)
            STA[...] = jnp.where(stage_a() == 0, X[X1, 0, 0:F // 2], X[X1, 1, 0:F // 2])
            STB[...] = jnp.where(stage_b() == 0, X[Z1, 0, F // 2:F], X[Z1, 1, F // 2:F])
            for item in diagonal_copies():
                item.start()

        @pl.when(step == 3)
        def _():
            arrived(TAB, X2)
            table_back().start()
            for kind in SMALL + BULK:
                arrived(kind, SIB)

            @pl.when(k == 0)
            def _():
                second_y().wait_recv()

            for kind in (SQ, SUB):
                arrived(kind, Y2)

        @pl.when(jnp.logical_and(step == 4, k == 0))
        def _():
            for item in next_y():
                item.wait_recv()

        @pl.when(jnp.logical_and(step == 4, k == 1))
        def _():
            second_y().wait_recv()

        pairs = [pair_of(step, place) for place in range(2)]
        add_terms(pairs, [tile(*pair) for pair in pairs], step == 0)
        return carry

    lax.fori_loop(0, len(STEPS) - 1 + takes_y.astype(jnp.int32), step_body, 0)
    for slot in (Y1, SIB, Y2):
        start_back(slot)

    @pl.when(jnp.logical_and(k == 0, takes_y))
    def _():
        start_back(YN)

    for slot, kinds in ((X2, (SQ, SUB, M0, M1)), (Z2, SMALL + (M0, M1))):
        for kind in kinds:
            arrived(kind, slot)
    head, rest = slice(0, CUT), slice(CUT, F)

    def early_body(step, carry):
        for place in range(2):
            i, j, bi, _, at = last_pair_of(step, place)
            G[2 * step + place] = inner_of(i, j, bi, at, head)
        return carry

    lax.fori_loop(0, len(LAST_STEPS), early_body, 0)
    for kind in (N0, N1):
        for slot in (X2, Z2):
            arrived(kind, slot)

    def last_body(step, carry):
        pairs = [last_pair_of(step, place) for place in range(2)]
        kernels = []
        for place, (i, j, bi, bj, at) in enumerate(pairs):
            kernels.append(kernel_of(G[2 * step + place] + inner_of(i, j, bi, at, rest), i, j, bi, bj))
        add_terms(pairs, kernels, False)

        @pl.when(step == 0)
        def _():
            start_back(X1)
            start_back(Z1)

        return carry

    lax.fori_loop(0, len(LAST_STEPS), last_body, 0)
    start_back(X2)
    start_back(Z2)
    for item in diagonal_copies():
        item.wait_recv()
    bi, bj = chosen(OWN, DG, 2 * r, 2 * row_at(-1, -1))
    kernel = tile(OWN, DG, bi, bj, 0)
    BACK[DG - 1, 0] = jnp.where(bj >= 0, right_part(kernel, OWN, bi), 0.0).astype(BF16)
    give_back(DG).start()
    for_left = left_part(kernel, DG, bj)
    total = [ACC[OWN, b] + jnp.where(bi == b, for_left, 0.0) for b in range(2)]

    for path in paths:
        for kind in SMALL if path[0] == 6 else SMALL + BULK:
            copy(path[0], kind, *path[1:]).wait_send()

    @pl.when(jnp.logical_or(k == 0, next_takes))
    def _():
        second_y().wait_send()

    @pl.when(jnp.logical_and(k == 0, last_takes))
    def _():
        for item in next_y():
            item.wait_send()

    @pl.when(k == 1)
    def _():
        sibling_table().wait_send()

    for kind in SMALL + BULK:
        copy(3, kind, OWN, SIB, sibling).wait_send()
    copy(9, TAB, OWN, TAB_Z, on_row(0, -1)).wait_send()
    copy(10, TAB, OWN, TAB_X, on_row(-1, 0)).wait_send()
    copy(11, TAB, OWN, TAB_Y, on_col(-1)).wait_send()
    for item in diagonal_copies():
        item.wait_send()
    for slot in (Y1, X1, Z1, X2, SIB, Y2, Z2):
        give_back(slot).wait()
        for b in range(2):
            total[b] = total[b] + RET[slot - 1, b].astype(F32)

    @pl.when(jnp.logical_and(k == 0, takes_y))
    def _():
        give_back(YN).wait_send()

    given = jnp.logical_and(k == 0, last_takes)

    @pl.when(given)
    def _():
        give_back(YN).wait_recv()

    @pl.when(jnp.logical_not(given))
    def _():
        RET[YN - 1] = jnp.zeros((2, COLS, BS), BF16)

    total = [total[b] + RET[YN - 1, b].astype(F32) for b in range(2)]
    table_back().wait()
    mine = jnp.maximum(T[OWN, 2 * row_at(1, 1)], T[TAB_D, 2 * r + 1])
    give_back(DG).wait()
    last = RET[DG - 1, 0].astype(F32)
    for b in range(2):
        out[b] = total[b] + jnp.where(mine == b, last, 0.0)


def body(histograms, basis, row_pairs, col_pairs):
    return pl.pallas_call(
        item_kernel,
        out_shape=jax.ShapeDtypeStruct((2, COLS, BS), F32),
        in_specs=[
            pl.BlockSpec(memory_space=pl.ANY),
            pl.BlockSpec(memory_space=pl.ANY),
            pl.BlockSpec(memory_space=pltpu.SMEM),
            pl.BlockSpec(memory_space=pltpu.SMEM),
        ],
        out_specs=pl.BlockSpec(memory_space=pltpu.VMEM),
        scratch_shapes=[
            pltpu.VMEM((SLOTS, 2, F, BS), BF16),
            pltpu.VMEM((SLOTS, 2, COLS, BS), BF16),
            pltpu.VMEM((SLOTS, 8, BS), F32),
            pltpu.SMEM((15, 48), jnp.int32),
            pltpu.VMEM((SLOTS, 2, COLS, BS), F32),
            pltpu.VMEM((SLOTS - 1, 2, COLS, BS), BF16),
            pltpu.VMEM((SLOTS - 1, 2, COLS, BS), BF16),
            pltpu.VMEM((F // 2, BS), BF16),
            pltpu.VMEM((F // 2, BS), BF16),
            pltpu.VMEM((2, F, BS), BF16),
            pltpu.VMEM((4, BS, BS), F32),
            pltpu.SemaphoreType.DMA((3,)),
            pltpu.SemaphoreType.DMA((15, 7)),
            pltpu.SemaphoreType.DMA((15, 7)),
            pltpu.SemaphoreType.DMA((SLOTS - 1,)),
            pltpu.SemaphoreType.DMA((SLOTS - 1,)),
        ],
        compiler_params=pltpu.CompilerParams(
            collective_id=0, has_side_effects=True, vmem_limit_bytes=56 * 1024 * 1024
        ),
    )(jnp.swapaxes(histograms, 1, 2), basis, jnp.swapaxes(row_pairs, 1, 2), jnp.swapaxes(col_pairs, 1, 2))


def solution(mesh):
    spec = P(("row", "col"), None, None)
    return jax.shard_map(body, mesh=mesh, in_specs=(spec,) * 4, out_specs=spec, check_vma=False)
```

```python
import jax
import jax.numpy as jnp
from jax import lax
from jax.experimental import pallas as pl
from jax.experimental.pallas import tpu as pltpu
from jax.sharding import PartitionSpec as P

F = 672
BS = 640
COLS = 32
SCALE = 1.4426950408889634 / (0.09 * F)
MESH = pl.DeviceIdType.MESH
NT = (((1,), (1,)), ((), ()))
TN = (((0,), (0,)), ((), ()))
F32 = jnp.float32
BF16 = jnp.bfloat16

OWN, X1, X2, Z1, Z2, Y1, Y2, SIB, DG, YN = range(10)
TAB_Z, TAB_X, TAB_D, TAB_Y, TAB_S = range(10, 15)
SLOTS = 10
M0, M1, N0, N1, SUB, SQ, TAB = range(7)
BULK, SMALL = (M0, M1, N0, N1), (TAB, SQ, SUB)
HALF = 352
CUT = 512

STEPS = [
    ((0, 0), (0, 0)),
    ((0, 1), (0, 3)),
    ((1, 3), (0, 5)),
    ((7, 5), (0, 7)),
    ((0, 6), (0, 0)),
]
COL_PAIRS = ((2, 1), (3, 0), (3, 1), (4, 0))
LAST_STEPS = [
    ((1, 4), (2, 3)),
    ((0, 2), (0, 4)),
]


def pick(index, values):
    result = values[-1]
    for position in range(len(values) - 2, -1, -1):
        result = jnp.where(index == position, values[position], result)
    return result


def item_kernel(hist, basis, row_table, col_table, out, X, B, Q, T, ACC, BACK, RET, STA, STB, STC, STE, G,
                in_sem, send_sem, recv_sem, back_send, back_recv):
    r = lax.axis_index("row")
    c = lax.axis_index("col")
    z, x, y, k = r // 4, lax.rem(r, 4), c // 2, lax.rem(c, 2)
    s = 1 - 2 * k

    def row_at(dx, dz):
        return lax.rem(z + s * dz + 8, 4) * 4 + lax.rem(x + s * dx + 8, 4)

    def col_at(dy):
        return lax.rem(y + s * dy + 8, 4) * 2 + k

    def on_row(dx, dz):
        return (row_at(dx, dz), c)

    def on_col(dy):
        return (r, col_at(dy))

    sibling = (r, y * 2 + 1 - k)
    cross = (r, lax.rem(y + s + 4, 4) * 2 + 1 - k)
    sib_next_col = lax.rem(y + 2, 4) * 2 + 1 - k
    sib_owner_col = jnp.where(k == 0, cross[1], sibling[1])

    barrier = pltpu.get_barrier_semaphore()
    sources = [on_row(-1, 0), on_row(0, -1), on_col(-1), sibling]
    for source in sources:
        pl.semaphore_signal(barrier, inc=1, device_id=source, device_id_type=MESH)

    copies_in = [pltpu.make_async_copy(hist.at[b], X.at[OWN, b], in_sem.at[b]) for b in range(2)]
    copies_in.append(pltpu.make_async_copy(basis, B.at[OWN], in_sem.at[2]))
    for item in copies_in:
        item.start()

    ACC[...] = jnp.zeros_like(ACC)

    def load_table(i, carry):
        T[OWN, 2 * i] = row_table[0, 0, i]
        T[OWN, 2 * i + 1] = row_table[0, 1, i]
        return carry

    lax.fori_loop(0, 16, load_table, 0)

    def load_col(i, carry):
        T[OWN, 32 + 2 * i] = col_table[0, 0, i]
        T[OWN, 33 + 2 * i] = col_table[0, 1, i]
        return carry

    lax.fori_loop(0, 8, load_col, 0)

    for item in copies_in:
        item.wait()
    for b in range(2):
        values = X[OWN, b].astype(F32)
        Q[OWN, b:b + 1] = jnp.sum(values * values, axis=0, keepdims=True) * (-SCALE)

    pl.semaphore_wait(barrier, len(sources))

    def remote(src, dst, send, recv, device):
        return pltpu.make_async_remote_copy(src_ref=src, dst_ref=dst, send_sem=send, recv_sem=recv,
                                            device_id=device, device_id_type=MESH)

    def part(kind, slot):
        if kind in BULK:
            return X.at[slot, kind % 2, pl.ds(0, CUT) if kind < 2 else pl.ds(CUT, F - CUT)]
        return {SUB: B, SQ: Q, TAB: T}[kind].at[slot]

    def copy(path, kind, src, dst, device):
        return remote(part(kind, src), part(kind, dst), send_sem.at[path, kind], recv_sem.at[dst, kind], device)

    def arrived(kind, slot):
        copy(0, kind, slot, slot, sibling).wait_recv()

    paths = [(0, OWN, X1, on_row(1, 0)), (1, OWN, Z1, on_row(0, 1)), (2, OWN, Y1, on_col(1)),
             (4, X1, X2, on_row(1, 0)), (5, Z1, Z2, on_row(0, 1)), (6, Y1, Y2, on_col(1))]

    def send_own(kind):
        for path in paths[:3]:
            copy(path[0], kind, *path[1:]).start()

        @pl.when(k == 0)
        def _():
            copy(3, kind, OWN, SIB, sibling).start()

    for kind in SMALL + (M0, M1):
        send_own(kind)

    def row_of(slot):
        return pick(slot, [r, row_at(-1, 0), row_at(-2, 0), row_at(0, -1), row_at(0, -2), r, r, r, row_at(-1, -1), r])

    def col_of(slot):
        return pick(slot, [c, c, c, c, c, col_at(-1), col_at(-2), sib_owner_col, c, col_at(1)])

    def chosen(i, j, ki, kj):
        return jnp.maximum(T[i, kj], T[j, ki + 1]), jnp.maximum(T[i, kj + 1], T[j, ki])

    def stage_a():
        target, owner = 2 * row_at(0, 1), 2 * row_at(-1, 0)
        return jnp.maximum(T[X1, target], T[TAB_Z, owner + 1])

    def stage_b():
        target, owner = 2 * row_at(1, 0), 2 * row_at(0, -1)
        return jnp.maximum(T[Z1, target], T[TAB_X, owner + 1])

    def stage_cross():
        return jnp.maximum(T[Y1, 32 + 2 * sib_next_col], T[TAB_S, 33 + 2 * col_at(-1)])

    def stage_far():
        return jnp.maximum(T[Y1, 32 + 2 * col_at(1)], T[TAB_Y, 33 + 2 * col_at(-1)])

    def stage_back():
        return jnp.maximum(T[OWN, 32 + 2 * col_at(-2)], T[Y2, 33 + 2 * c])

    def second_y():
        return remote(STC.at[0], X.at[Y2, 0], send_sem.at[6, M0], recv_sem.at[Y2, M0], on_col(1))

    def next_y():
        return [copy(13, kind, OWN, YN, on_col(-1)) for kind in SMALL] + [
            remote(STC.at[1], X.at[YN, 0], send_sem.at[13, M0], recv_sem.at[YN, M0], on_col(-1))]

    def sibling_table():
        return remote(T.at[Y2], T.at[TAB_S], send_sem.at[12, TAB], recv_sem.at[TAB_S, TAB], sibling)

    first, second = pl.ds(0, HALF), pl.ds(HALF, F - HALF)
    to_z, to_x = on_row(0, 1), on_row(1, 0)

    def diagonal_copies():
        return [
            copy(7, TAB, X1, DG, to_z),
            copy(7, SQ, X1, DG, to_z),
            remote(STE, B.at[DG, 0], send_sem.at[8, SUB], recv_sem.at[DG, SUB], to_x),
            remote(STA, X.at[DG, 0, first], send_sem.at[7, M0], recv_sem.at[DG, M0], to_z),
            remote(STB, X.at[DG, 0, second], send_sem.at[8, M1], recv_sem.at[DG, M1], to_x),
        ]

    owners = [None, on_row(-1, 0), on_row(-2, 0), on_row(0, -1), on_row(0, -2), on_col(-1), on_col(-2),
              (r, sib_owner_col), on_row(-1, -1), on_col(1)]

    def give_back(slot):
        part = (slot - 1, 0) if slot == DG else slot - 1
        return remote(BACK.at[part], RET.at[part], back_send.at[slot - 1], back_recv.at[slot - 1], owners[slot])

    def table_back():
        return remote(T.at[OWN], T.at[TAB_D], send_sem.at[7, M1], recv_sem.at[TAB_D, TAB], owners[DG])

    def start_back(slot):
        BACK[slot - 1] = ACC[slot].astype(BF16)
        give_back(slot).start()

    west = x < 2

    def takes(dy):
        return ((z < 2) == (lax.rem(y + s * dy + 4, 4) < 2)) == (k == 1)

    takes_y, next_takes, last_takes = takes(0), takes(1), takes(-1)

    def pair_of(step, place):
        i, j = [pick(step, [entry[place][side] for entry in STEPS]) for side in range(2)]
        along_col = step < 0
        for s_col, p_col in COL_PAIRS:
            if p_col == place:
                along_col = jnp.logical_or(along_col, step == s_col)
        if place == 0:
            swap = jnp.logical_and(step == 4, k == 0)
            i, j = jnp.where(swap, Y1, i), jnp.where(swap, YN, j)
        else:
            swap = jnp.logical_and(step == 3, k == 0)
            i, j = jnp.where(swap, SIB, i), jnp.where(swap, Y2, j)
        ki = jnp.where(along_col, 32 + 2 * col_of(i), 2 * row_of(i))
        kj = jnp.where(along_col, 32 + 2 * col_of(j), 2 * row_of(j))
        bi, bj = chosen(i, j, ki, kj)
        diagonal = step == 0
        bi, bj = jnp.where(diagonal, place, bi), jnp.where(diagonal, place, bj)
        if place == 1:
            bi, bj = jnp.where(step == 4, -1, bi), jnp.where(step == 4, -1, bj)
        at = jnp.where(jnp.logical_or(j == Y2, j == YN), 0, bj)
        return i, j, bi, bj, at

    def last_pair_of(step, place):
        i, j = [pick(step, [entry[place][side] for entry in LAST_STEPS]) for side in range(2)]
        if place == 0:
            swap = jnp.logical_and(step == 1, jnp.logical_not(west))
            i, j = jnp.where(swap, X2, i), jnp.where(swap, Z2, j)
        bi, bj = chosen(i, j, 2 * row_of(i), 2 * row_of(j))
        if place == 1:
            left_out = jnp.logical_and(step == 1, takes_y)
            bi, bj = jnp.where(left_out, -1, bi), jnp.where(left_out, -1, bj)
        return i, j, bi, bj, bj

    def inner_of(i, j, bi, at, rows):
        left = jnp.where(bi == 0, X[i, 0, rows], X[i, 1, rows])
        right = X[j, at, rows] if isinstance(at, int) else jnp.where(at == 0, X[j, 0, rows], X[j, 1, rows])
        return lax.dot_general(left, right, TN, preferred_element_type=F32)

    def kernel_of(inner, i, j, bi, bj):
        left_squares = jnp.where(bi == 0, Q[i, 0:1], Q[i, 1:2])
        right_squares = jnp.where(bj == 0, Q[j, 0:1], Q[j, 1:2])
        squares = jnp.broadcast_to(left_squares, (8, BS)).T[:, 0:1] + right_squares
        return jnp.exp2(jnp.minimum(inner * (2 * SCALE) + squares, 0.0)).astype(BF16)

    def tile(i, j, bi, bj, at):
        return kernel_of(inner_of(i, j, bi, at, slice(None)), i, j, bi, bj)

    def add_terms(pairs, kernels, diagonal):
        for (i, j, bi, bj, _), kernel in zip(pairs, kernels):
            for_left, for_right = left_part(kernel, j, bj), right_part(kernel, i, bi)
            for b in range(2):
                ACC[i, b] += jnp.where(jnp.logical_and(bi == b, jnp.logical_not(diagonal)), for_left, 0.0)
                ACC[j, b] += jnp.where(bj == b, for_right, 0.0)

    def left_part(kernel, j, bj):
        right_basis = jnp.where(bj == 0, B[j, 0], B[j, 1])
        return lax.dot_general(kernel, right_basis, NT, preferred_element_type=F32).T

    def right_part(kernel, i, bi):
        return jnp.dot(jnp.where(bi == 0, B[i, 0], B[i, 1]), kernel, preferred_element_type=F32)

    def step_body(step, carry):
        @pl.when(step == 0)
        def _():
            for slot in (X1, Z1, Y1):
                for kind in SMALL:
                    arrived(kind, slot)
            copy(9, TAB, OWN, TAB_Z, on_row(0, -1)).start()
            copy(10, TAB, OWN, TAB_X, on_row(-1, 0)).start()
            copy(11, TAB, OWN, TAB_Y, on_col(-1)).start()
            for kind in SMALL:
                for path in paths[3:]:
                    copy(path[0], kind, *path[1:]).start()

                @pl.when(k == 1)
                def _():
                    copy(3, kind, Y1, SIB, sibling).start()

            for kind in BULK[2:]:
                send_own(kind)

            @pl.when(k == 1)
            def _():
                arrived(TAB, Y2)
                sibling_table().start()

            for kind in BULK:
                for slot, path in zip((X1, Z1), paths[3:]):
                    arrived(kind, slot)
                    copy(path[0], kind, *path[1:]).start()
                arrived(kind, Y1)

                @pl.when(k == 1)
                def _():
                    copy(3, kind, Y1, SIB, sibling).start()
            arrived(TAB, TAB_Y)

            @pl.when(k == 0)
            def _():
                arrived(TAB, TAB_S)
                STC[0] = jnp.where(stage_cross() == 0, X[Y1, 0], X[Y1, 1])
                second_y().start()

            @pl.when(k == 0)
            def _():
                arrived(TAB, Y2)

            @pl.when(jnp.logical_and(k == 0, last_takes))
            def _():
                STC[1] = jnp.where(stage_back() == 0, X[OWN, 0], X[OWN, 1])
                for item in next_y():
                    item.start()

            @pl.when(jnp.logical_and(k == 1, next_takes))
            def _():
                STC[0] = jnp.where(stage_far() == 0, X[Y1, 0], X[Y1, 1])
                second_y().start()

            arrived(TAB, TAB_Z)
            arrived(TAB, TAB_X)
            STA[...] = jnp.where(stage_a() == 0, X[X1, 0, 0:HALF], X[X1, 1, 0:HALF])
            STB[...] = jnp.where(stage_b() == 0, X[Z1, 0, HALF:F], X[Z1, 1, HALF:F])
            STE[...] = jnp.where(stage_b() == 0, B[Z1, 0], B[Z1, 1])
            for item in diagonal_copies():
                item.start()

        @pl.when(step == 3)
        def _():
            arrived(TAB, X2)
            table_back().start()
            for kind in SMALL + BULK:
                arrived(kind, SIB)

            @pl.when(k == 0)
            def _():
                second_y().wait_recv()

            for kind in (SQ, SUB):
                arrived(kind, Y2)

        @pl.when(jnp.logical_and(step == 4, k == 0))
        def _():
            for item in next_y():
                item.wait_recv()

        @pl.when(jnp.logical_and(step == 4, k == 1))
        def _():
            second_y().wait_recv()

        pairs = [pair_of(step, place) for place in range(2)]
        add_terms(pairs, [tile(*pair) for pair in pairs], step == 0)
        return carry

    lax.fori_loop(0, len(STEPS) - 1 + takes_y.astype(jnp.int32), step_body, 0)
    for slot in (Y1, SIB, Y2):
        start_back(slot)

    @pl.when(jnp.logical_and(k == 0, takes_y))
    def _():
        start_back(YN)

    for slot, kinds in ((X2, (SQ, SUB, M0, M1)), (Z2, SMALL + (M0, M1))):
        for kind in kinds:
            arrived(kind, slot)
    head, rest = slice(0, CUT), slice(CUT, F)

    def early_body(step, carry):
        for place in range(2):
            i, j, bi, _, at = last_pair_of(step, place)
            G[2 * step + place] = inner_of(i, j, bi, at, head)
        return carry

    lax.fori_loop(0, len(LAST_STEPS), early_body, 0)
    for kind in (N0, N1):
        for slot in (X2, Z2):
            arrived(kind, slot)

    def last_body(step, carry):
        pairs = [last_pair_of(step, place) for place in range(2)]
        kernels = []
        for place, (i, j, bi, bj, at) in enumerate(pairs):
            kernels.append(kernel_of(G[2 * step + place] + inner_of(i, j, bi, at, rest), i, j, bi, bj))
        add_terms(pairs, kernels, False)

        @pl.when(step == 0)
        def _():
            start_back(X1)
            start_back(Z1)

        return carry

    lax.fori_loop(0, len(LAST_STEPS), last_body, 0)
    start_back(X2)
    start_back(Z2)
    for item in diagonal_copies():
        item.wait_recv()
    bi, bj = chosen(OWN, DG, 2 * r, 2 * row_at(-1, -1))
    kernel = tile(OWN, DG, bi, bj, 0)
    BACK[DG - 1, 0] = jnp.where(bj >= 0, right_part(kernel, OWN, bi), 0.0).astype(BF16)
    give_back(DG).start()
    for_left = left_part(kernel, DG, 0)
    total = [ACC[OWN, b] + jnp.where(bi == b, for_left, 0.0) for b in range(2)]

    for path in paths:
        for kind in SMALL if path[0] == 6 else SMALL + BULK:
            copy(path[0], kind, *path[1:]).wait_send()

    @pl.when(jnp.logical_or(k == 0, next_takes))
    def _():
        second_y().wait_send()

    @pl.when(jnp.logical_and(k == 0, last_takes))
    def _():
        for item in next_y():
            item.wait_send()

    @pl.when(k == 1)
    def _():
        sibling_table().wait_send()

    for kind in SMALL + BULK:
        copy(3, kind, OWN, SIB, sibling).wait_send()
    copy(9, TAB, OWN, TAB_Z, on_row(0, -1)).wait_send()
    copy(10, TAB, OWN, TAB_X, on_row(-1, 0)).wait_send()
    copy(11, TAB, OWN, TAB_Y, on_col(-1)).wait_send()
    for item in diagonal_copies():
        item.wait_send()
    for slot in (Y1, X1, Z1, X2, SIB, Y2, Z2):
        give_back(slot).wait()
        for b in range(2):
            total[b] = total[b] + RET[slot - 1, b].astype(F32)

    @pl.when(jnp.logical_and(k == 0, takes_y))
    def _():
        give_back(YN).wait_send()

    given = jnp.logical_and(k == 0, last_takes)

    @pl.when(given)
    def _():
        give_back(YN).wait_recv()

    @pl.when(jnp.logical_not(given))
    def _():
        RET[YN - 1] = jnp.zeros((2, COLS, BS), BF16)

    total = [total[b] + RET[YN - 1, b].astype(F32) for b in range(2)]
    table_back().wait()
    mine = jnp.maximum(T[OWN, 2 * row_at(1, 1)], T[TAB_D, 2 * r + 1])
    give_back(DG).wait()
    last = RET[DG - 1, 0].astype(F32)
    for b in range(2):
        out[b] = total[b] + jnp.where(mine == b, last, 0.0)


def body(histograms, basis, row_pairs, col_pairs):
    return pl.pallas_call(
        item_kernel,
        out_shape=jax.ShapeDtypeStruct((2, COLS, BS), F32),
        in_specs=[
            pl.BlockSpec(memory_space=pl.ANY),
            pl.BlockSpec(memory_space=pl.ANY),
            pl.BlockSpec(memory_space=pltpu.SMEM),
            pl.BlockSpec(memory_space=pltpu.SMEM),
        ],
        out_specs=pl.BlockSpec(memory_space=pltpu.VMEM),
        scratch_shapes=[
            pltpu.VMEM((SLOTS, 2, F, BS), BF16),
            pltpu.VMEM((SLOTS, 2, COLS, BS), BF16),
            pltpu.VMEM((SLOTS, 2, BS), F32),
            pltpu.SMEM((15, 48), jnp.int32),
            pltpu.VMEM((SLOTS, 2, COLS, BS), F32),
            pltpu.VMEM((SLOTS - 1, 2, COLS, BS), BF16),
            pltpu.VMEM((SLOTS - 1, 2, COLS, BS), BF16),
            pltpu.VMEM((HALF, BS), BF16),
            pltpu.VMEM((F - HALF, BS), BF16),
            pltpu.VMEM((2, F, BS), BF16),
            pltpu.VMEM((COLS, BS), BF16),
            pltpu.VMEM((4, BS, BS), F32),
            pltpu.SemaphoreType.DMA((3,)),
            pltpu.SemaphoreType.DMA((15, 7)),
            pltpu.SemaphoreType.DMA((15, 7)),
            pltpu.SemaphoreType.DMA((SLOTS - 1,)),
            pltpu.SemaphoreType.DMA((SLOTS - 1,)),
        ],
        compiler_params=pltpu.CompilerParams(
            collective_id=0, has_side_effects=True, vmem_limit_bytes=56 * 1024 * 1024
        ),
    )(jnp.swapaxes(histograms, 1, 2), basis, jnp.swapaxes(row_pairs, 1, 2), jnp.swapaxes(col_pairs, 1, 2))


def solution(mesh):
    spec = P(("row", "col"), None, None)
    return jax.shard_map(body, mesh=mesh, in_specs=(spec,) * 4, out_specs=spec, check_vma=False)
```

```python
import jax
import jax.numpy as jnp
from jax import lax
from jax.experimental import pallas as pl
from jax.experimental.pallas import tpu as pltpu
from jax.sharding import PartitionSpec as P

F = 672
BS = 640
COLS = 32
SCALE = 1.4426950408889634 / (0.09 * F)
MESH = pl.DeviceIdType.MESH
NT = (((1,), (1,)), ((), ()))
TN = (((0,), (0,)), ((), ()))
F32 = jnp.float32
BF16 = jnp.bfloat16

OWN, X1, X2, Z1, Z2, Y1, Y2, SIB, DG, YN = range(10)
TAB_Z, TAB_X, TAB_D, TAB_Y, TAB_S = range(10, 15)
SLOTS = 10
HEAD, REST, SUB, SQ, TAB = range(5)
BULK, SMALL = (HEAD, REST), (TAB, SQ, SUB)
HALF = 352
CUT = 512

STEPS = [
    ((0, 0), (0, 0)),
    ((0, 1), (0, 3)),
    ((1, 3), (0, 5)),
    ((7, 5), (0, 7)),
    ((0, 6), (0, 0)),
]
COL_PAIRS = ((2, 1), (3, 0), (3, 1), (4, 0))
LAST_STEPS = [
    ((1, 4), (2, 3)),
    ((0, 2), (0, 4)),
]


def pick(index, values):
    result = values[-1]
    for position in range(len(values) - 2, -1, -1):
        result = jnp.where(index == position, values[position], result)
    return result


def item_kernel(hist, basis, row_table, col_table, out, X, B, Q, T, ACC, BACK, RET, STA, STB, STC, STE, G, RT, CT,
                in_sem, send_sem, recv_sem, back_send, back_recv):
    r = lax.axis_index("row")
    c = lax.axis_index("col")
    z, x, y, k = r // 4, lax.rem(r, 4), c // 2, lax.rem(c, 2)
    s = 1 - 2 * k

    def row_at(dx, dz):
        return lax.rem(z + s * dz + 8, 4) * 4 + lax.rem(x + s * dx + 8, 4)

    def col_at(dy):
        return lax.rem(y + s * dy + 8, 4) * 2 + k

    def on_row(dx, dz):
        return (row_at(dx, dz), c)

    def on_col(dy):
        return (r, col_at(dy))

    sibling = (r, y * 2 + 1 - k)
    cross = (r, lax.rem(y + s + 4, 4) * 2 + 1 - k)
    sib_next_col = lax.rem(y + 2, 4) * 2 + 1 - k
    sib_owner_col = jnp.where(k == 0, cross[1], sibling[1])

    barrier = pltpu.get_barrier_semaphore()
    sources = [on_row(-1, 0), on_row(0, -1), on_col(-1), sibling]
    for source in sources:
        pl.semaphore_signal(barrier, inc=1, device_id=source, device_id_type=MESH)

    copies_in = [pltpu.make_async_copy(hist.at[b], X.at[OWN, b], in_sem.at[b]) for b in range(2)]
    copies_in.append(pltpu.make_async_copy(basis, B.at[OWN], in_sem.at[2]))
    tables_in = [pltpu.make_async_copy(row_table, RT, in_sem.at[3]), pltpu.make_async_copy(col_table, CT, in_sem.at[4])]
    for item in tables_in + copies_in:
        item.start()

    ACC[...] = jnp.zeros_like(ACC)

    for item in tables_in:
        item.wait()

    def load_table(i, carry):
        T[OWN, 2 * i] = RT[0, 0, i]
        T[OWN, 2 * i + 1] = RT[0, 1, i]
        return carry

    lax.fori_loop(0, 16, load_table, 0)

    def load_col(i, carry):
        T[OWN, 32 + 2 * i] = CT[0, 0, i]
        T[OWN, 33 + 2 * i] = CT[0, 1, i]
        return carry

    lax.fori_loop(0, 8, load_col, 0)

    for item in copies_in:
        item.wait()
    for b in range(2):
        values = X[OWN, b].astype(F32)
        Q[OWN, b:b + 1] = jnp.sum(values * values, axis=0, keepdims=True) * (-SCALE)

    pl.semaphore_wait(barrier, len(sources))

    def remote(src, dst, send, recv, device):
        return pltpu.make_async_remote_copy(src_ref=src, dst_ref=dst, send_sem=send, recv_sem=recv,
                                            device_id=device, device_id_type=MESH)

    def part(kind, slot):
        if kind in BULK:
            return X.at[slot, :, pl.ds(0, CUT) if kind == HEAD else pl.ds(CUT, F - CUT)]
        return {SUB: B, SQ: Q, TAB: T}[kind].at[slot]

    def copy(path, kind, src, dst, device):
        return remote(part(kind, src), part(kind, dst), send_sem.at[path, kind], recv_sem.at[dst, kind], device)

    def arrived(kind, slot):
        copy(0, kind, slot, slot, sibling).wait_recv()

    paths = [(0, OWN, X1, on_row(1, 0)), (1, OWN, Z1, on_row(0, 1)), (2, OWN, Y1, on_col(1)),
             (4, X1, X2, on_row(1, 0)), (5, Z1, Z2, on_row(0, 1)), (6, Y1, Y2, on_col(1))]

    def send_own(kind):
        for path in paths[:3]:
            copy(path[0], kind, *path[1:]).start()

        @pl.when(k == 0)
        def _():
            copy(3, kind, OWN, SIB, sibling).start()

    for kind in SMALL + (HEAD,):
        send_own(kind)

    def row_of(slot):
        return pick(slot, [r, row_at(-1, 0), row_at(-2, 0), row_at(0, -1), row_at(0, -2), r, r, r, row_at(-1, -1), r])

    def col_of(slot):
        return pick(slot, [c, c, c, c, c, col_at(-1), col_at(-2), sib_owner_col, c, col_at(1)])

    def chosen(i, j, ki, kj):
        return jnp.maximum(T[i, kj], T[j, ki + 1]), jnp.maximum(T[i, kj + 1], T[j, ki])

    def stage_a():
        target, owner = 2 * row_at(0, 1), 2 * row_at(-1, 0)
        return jnp.maximum(T[X1, target], T[TAB_Z, owner + 1])

    def stage_b():
        target, owner = 2 * row_at(1, 0), 2 * row_at(0, -1)
        return jnp.maximum(T[Z1, target], T[TAB_X, owner + 1])

    def stage_cross():
        return jnp.maximum(T[Y1, 32 + 2 * sib_next_col], T[TAB_S, 33 + 2 * col_at(-1)])

    def stage_far():
        return jnp.maximum(T[Y1, 32 + 2 * col_at(1)], T[TAB_Y, 33 + 2 * col_at(-1)])

    def stage_back():
        return jnp.maximum(T[OWN, 32 + 2 * col_at(-2)], T[Y2, 33 + 2 * c])

    def second_y():
        return remote(STC.at[0], X.at[Y2, 0], send_sem.at[6, HEAD], recv_sem.at[Y2, HEAD], on_col(1))

    def next_y():
        return [copy(13, kind, OWN, YN, on_col(-1)) for kind in SMALL] + [
            remote(STC.at[1], X.at[YN, 0], send_sem.at[13, HEAD], recv_sem.at[YN, HEAD], on_col(-1))]

    def sibling_table():
        return remote(T.at[Y2], T.at[TAB_S], send_sem.at[12, TAB], recv_sem.at[TAB_S, TAB], sibling)

    first, second = pl.ds(0, HALF), pl.ds(HALF, F - HALF)
    to_z, to_x = on_row(0, 1), on_row(1, 0)

    def diagonal_copies():
        return [
            copy(7, TAB, X1, DG, to_z),
            copy(7, SQ, X1, DG, to_z),
            remote(STE, B.at[DG, 0], send_sem.at[8, SUB], recv_sem.at[DG, SUB], to_x),
            remote(STA, X.at[DG, 0, first], send_sem.at[7, HEAD], recv_sem.at[DG, HEAD], to_z),
            remote(STB, X.at[DG, 0, second], send_sem.at[8, REST], recv_sem.at[DG, REST], to_x),
        ]

    owners = [None, on_row(-1, 0), on_row(-2, 0), on_row(0, -1), on_row(0, -2), on_col(-1), on_col(-2),
              (r, sib_owner_col), on_row(-1, -1), on_col(1)]

    def give_back(slot):
        part = (slot - 1, 0) if slot == DG else slot - 1
        return remote(BACK.at[part], RET.at[part], back_send.at[slot - 1], back_recv.at[slot - 1], owners[slot])

    def table_back():
        return remote(T.at[OWN], T.at[TAB_D], send_sem.at[7, REST], recv_sem.at[TAB_D, TAB], owners[DG])

    def start_back(slot):
        BACK[slot - 1] = ACC[slot].astype(BF16)
        give_back(slot).start()

    west = x < 2

    def takes(dy):
        return ((z < 2) == (lax.rem(y + s * dy + 4, 4) < 2)) == (k == 1)

    takes_y, next_takes, last_takes = takes(0), takes(1), takes(-1)

    def pair_of(step, place):
        i, j = [pick(step, [entry[place][side] for entry in STEPS]) for side in range(2)]
        along_col = step < 0
        for s_col, p_col in COL_PAIRS:
            if p_col == place:
                along_col = jnp.logical_or(along_col, step == s_col)
        if place == 0:
            swap = jnp.logical_and(step == 4, k == 0)
            i, j = jnp.where(swap, Y1, i), jnp.where(swap, YN, j)
        else:
            swap = jnp.logical_and(step == 3, k == 0)
            i, j = jnp.where(swap, SIB, i), jnp.where(swap, Y2, j)
        ki = jnp.where(along_col, 32 + 2 * col_of(i), 2 * row_of(i))
        kj = jnp.where(along_col, 32 + 2 * col_of(j), 2 * row_of(j))
        bi, bj = chosen(i, j, ki, kj)
        diagonal = step == 0
        bi, bj = jnp.where(diagonal, place, bi), jnp.where(diagonal, place, bj)
        if place == 1:
            bi, bj = jnp.where(step == 4, -1, bi), jnp.where(step == 4, -1, bj)
        at = jnp.where(jnp.logical_or(j == Y2, j == YN), 0, bj)
        return i, j, bi, bj, at

    def last_pair_of(step, place):
        i, j = [pick(step, [entry[place][side] for entry in LAST_STEPS]) for side in range(2)]
        if place == 0:
            swap = jnp.logical_and(step == 1, jnp.logical_not(west))
            i, j = jnp.where(swap, X2, i), jnp.where(swap, Z2, j)
        bi, bj = chosen(i, j, 2 * row_of(i), 2 * row_of(j))
        if place == 1:
            left_out = jnp.logical_and(step == 1, takes_y)
            bi, bj = jnp.where(left_out, -1, bi), jnp.where(left_out, -1, bj)
        return i, j, bi, bj, bj

    def inner_of(i, j, bi, at, rows):
        left = jnp.where(bi == 0, X[i, 0, rows], X[i, 1, rows])
        right = X[j, at, rows] if isinstance(at, int) else jnp.where(at == 0, X[j, 0, rows], X[j, 1, rows])
        return lax.dot_general(left, right, TN, preferred_element_type=F32)

    def kernel_of(inner, i, j, bi, bj):
        left_squares = jnp.where(bi == 0, Q[i, 0:1], Q[i, 1:2])
        right_squares = jnp.where(bj == 0, Q[j, 0:1], Q[j, 1:2])
        squares = jnp.broadcast_to(left_squares, (8, BS)).T[:, 0:1] + right_squares
        return jnp.exp2(jnp.minimum(inner * (2 * SCALE) + squares, 0.0)).astype(BF16)

    def tile(i, j, bi, bj, at):
        return kernel_of(inner_of(i, j, bi, at, slice(None)), i, j, bi, bj)

    def add_terms(pairs, kernels, diagonal):
        for (i, j, bi, bj, _), kernel in zip(pairs, kernels):
            for_left, for_right = left_part(kernel, j, bj), right_part(kernel, i, bi)
            for b in range(2):
                ACC[i, b] += jnp.where(jnp.logical_and(bi == b, jnp.logical_not(diagonal)), for_left, 0.0)
                ACC[j, b] += jnp.where(bj == b, for_right, 0.0)

    def left_part(kernel, j, bj):
        right_basis = jnp.where(bj == 0, B[j, 0], B[j, 1])
        return lax.dot_general(kernel, right_basis, NT, preferred_element_type=F32).T

    def right_part(kernel, i, bi):
        return jnp.dot(jnp.where(bi == 0, B[i, 0], B[i, 1]), kernel, preferred_element_type=F32)

    def step_body(step, carry):
        @pl.when(step == 0)
        def _():
            for slot in (X1, Z1, Y1):
                for kind in SMALL:
                    arrived(kind, slot)
            copy(9, TAB, OWN, TAB_Z, on_row(0, -1)).start()
            copy(10, TAB, OWN, TAB_X, on_row(-1, 0)).start()
            copy(11, TAB, OWN, TAB_Y, on_col(-1)).start()
            for kind in SMALL:
                for path in paths[3:]:
                    copy(path[0], kind, *path[1:]).start()

                @pl.when(k == 1)
                def _():
                    copy(3, kind, Y1, SIB, sibling).start()

            send_own(REST)

            @pl.when(k == 1)
            def _():
                arrived(TAB, Y2)
                sibling_table().start()

            for kind in BULK:
                for slot, path in zip((X1, Z1), paths[3:]):
                    arrived(kind, slot)
                    copy(path[0], kind, *path[1:]).start()
                arrived(kind, Y1)

                @pl.when(k == 1)
                def _():
                    copy(3, kind, Y1, SIB, sibling).start()
            arrived(TAB, TAB_Y)

            @pl.when(k == 0)
            def _():
                arrived(TAB, TAB_S)
                STC[0] = jnp.where(stage_cross() == 0, X[Y1, 0], X[Y1, 1])
                second_y().start()

            @pl.when(k == 0)
            def _():
                arrived(TAB, Y2)

            @pl.when(jnp.logical_and(k == 0, last_takes))
            def _():
                STC[1] = jnp.where(stage_back() == 0, X[OWN, 0], X[OWN, 1])
                for item in next_y():
                    item.start()

            @pl.when(jnp.logical_and(k == 1, next_takes))
            def _():
                STC[0] = jnp.where(stage_far() == 0, X[Y1, 0], X[Y1, 1])
                second_y().start()

            arrived(TAB, TAB_Z)
            arrived(TAB, TAB_X)
            STA[...] = jnp.where(stage_a() == 0, X[X1, 0, 0:HALF], X[X1, 1, 0:HALF])
            STB[...] = jnp.where(stage_b() == 0, X[Z1, 0, HALF:F], X[Z1, 1, HALF:F])
            STE[...] = jnp.where(stage_b() == 0, B[Z1, 0], B[Z1, 1])
            for item in diagonal_copies():
                item.start()

        @pl.when(step == 3)
        def _():
            arrived(TAB, X2)
            table_back().start()
            for kind in SMALL + BULK:
                arrived(kind, SIB)

            @pl.when(k == 0)
            def _():
                second_y().wait_recv()

            for kind in (SQ, SUB):
                arrived(kind, Y2)

        @pl.when(jnp.logical_and(step == 4, k == 0))
        def _():
            for item in next_y():
                item.wait_recv()

        @pl.when(jnp.logical_and(step == 4, k == 1))
        def _():
            second_y().wait_recv()

        pairs = [pair_of(step, place) for place in range(2)]
        add_terms(pairs, [tile(*pair) for pair in pairs], step == 0)
        return carry

    lax.fori_loop(0, len(STEPS) - 1 + takes_y.astype(jnp.int32), step_body, 0)
    for slot in (Y1, SIB, Y2):
        start_back(slot)

    @pl.when(jnp.logical_and(k == 0, takes_y))
    def _():
        start_back(YN)

    for slot, kinds in ((X2, (SQ, SUB, HEAD)), (Z2, SMALL + (HEAD,))):
        for kind in kinds:
            arrived(kind, slot)
    head, rest = slice(0, CUT), slice(CUT, F)

    def early_body(step, carry):
        for place in range(2):
            i, j, bi, _, at = last_pair_of(step, place)
            G[2 * step + place] = inner_of(i, j, bi, at, head)
        return carry

    lax.fori_loop(0, len(LAST_STEPS), early_body, 0)
    for slot in (X2, Z2):
        arrived(REST, slot)

    def last_body(step, carry):
        pairs = [last_pair_of(step, place) for place in range(2)]
        kernels = []
        for place, (i, j, bi, bj, at) in enumerate(pairs):
            kernels.append(kernel_of(G[2 * step + place] + inner_of(i, j, bi, at, rest), i, j, bi, bj))
        add_terms(pairs, kernels, False)

        @pl.when(step == 0)
        def _():
            start_back(X1)
            start_back(Z1)

        return carry

    lax.fori_loop(0, len(LAST_STEPS), last_body, 0)
    start_back(X2)
    start_back(Z2)
    for item in diagonal_copies():
        item.wait_recv()
    bi, bj = chosen(OWN, DG, 2 * r, 2 * row_at(-1, -1))
    kernel = tile(OWN, DG, bi, bj, 0)
    BACK[DG - 1, 0] = jnp.where(bj >= 0, right_part(kernel, OWN, bi), 0.0).astype(BF16)
    give_back(DG).start()
    for_left = left_part(kernel, DG, 0)
    total = [ACC[OWN, b] + jnp.where(bi == b, for_left, 0.0) for b in range(2)]

    for path in paths:
        for kind in SMALL if path[0] == 6 else SMALL + BULK:
            copy(path[0], kind, *path[1:]).wait_send()

    @pl.when(jnp.logical_or(k == 0, next_takes))
    def _():
        second_y().wait_send()

    @pl.when(jnp.logical_and(k == 0, last_takes))
    def _():
        for item in next_y():
            item.wait_send()

    @pl.when(k == 1)
    def _():
        sibling_table().wait_send()

    for kind in SMALL + BULK:
        copy(3, kind, OWN, SIB, sibling).wait_send()
    copy(9, TAB, OWN, TAB_Z, on_row(0, -1)).wait_send()
    copy(10, TAB, OWN, TAB_X, on_row(-1, 0)).wait_send()
    copy(11, TAB, OWN, TAB_Y, on_col(-1)).wait_send()
    for item in diagonal_copies():
        item.wait_send()
    for slot in (Y1, X1, Z1, X2, SIB, Y2, Z2):
        give_back(slot).wait()
        for b in range(2):
            total[b] = total[b] + RET[slot - 1, b].astype(F32)

    @pl.when(jnp.logical_and(k == 0, takes_y))
    def _():
        give_back(YN).wait_send()

    given = jnp.logical_and(k == 0, last_takes)

    @pl.when(given)
    def _():
        give_back(YN).wait_recv()

    @pl.when(jnp.logical_not(given))
    def _():
        RET[YN - 1] = jnp.zeros((2, COLS, BS), BF16)

    total = [total[b] + RET[YN - 1, b].astype(F32) for b in range(2)]
    table_back().wait()
    mine = jnp.maximum(T[OWN, 2 * row_at(1, 1)], T[TAB_D, 2 * r + 1])
    give_back(DG).wait()
    last = RET[DG - 1, 0].astype(F32)
    for b in range(2):
        out[b] = total[b] + jnp.where(mine == b, last, 0.0)


def body(histograms, basis, row_pairs, col_pairs):
    return pl.pallas_call(
        item_kernel,
        out_shape=jax.ShapeDtypeStruct((2, COLS, BS), F32),
        in_specs=[
            pl.BlockSpec(memory_space=pl.ANY),
            pl.BlockSpec(memory_space=pl.ANY),
            pl.BlockSpec(memory_space=pl.ANY),
            pl.BlockSpec(memory_space=pl.ANY),
        ],
        out_specs=pl.BlockSpec(memory_space=pltpu.VMEM),
        scratch_shapes=[
            pltpu.VMEM((SLOTS, 2, F, BS), BF16),
            pltpu.VMEM((SLOTS, 2, COLS, BS), BF16),
            pltpu.VMEM((SLOTS, 2, BS), F32),
            pltpu.SMEM((15, 48), jnp.int32),
            pltpu.VMEM((SLOTS, 2, COLS, BS), F32),
            pltpu.VMEM((SLOTS - 1, 2, COLS, BS), BF16),
            pltpu.VMEM((SLOTS - 1, 2, COLS, BS), BF16),
            pltpu.VMEM((HALF, BS), BF16),
            pltpu.VMEM((F - HALF, BS), BF16),
            pltpu.VMEM((2, F, BS), BF16),
            pltpu.VMEM((COLS, BS), BF16),
            pltpu.VMEM((4, BS, BS), F32),
            pltpu.SMEM((1, 2, 16), jnp.int32),
            pltpu.SMEM((1, 2, 8), jnp.int32),
            pltpu.SemaphoreType.DMA((5,)),
            pltpu.SemaphoreType.DMA((15, 5)),
            pltpu.SemaphoreType.DMA((15, 5)),
            pltpu.SemaphoreType.DMA((SLOTS - 1,)),
            pltpu.SemaphoreType.DMA((SLOTS - 1,)),
        ],
        compiler_params=pltpu.CompilerParams(
            collective_id=0, has_side_effects=True, vmem_limit_bytes=56 * 1024 * 1024
        ),
    )(jnp.swapaxes(histograms, 1, 2), basis, jnp.swapaxes(row_pairs, 1, 2), jnp.swapaxes(col_pairs, 1, 2))


def solution(mesh):
    spec = P(("row", "col"), None, None)
    return jax.shard_map(body, mesh=mesh, in_specs=(spec,) * 4, out_specs=spec, check_vma=False)
```

```python
import jax
import jax.numpy as jnp
from jax import lax
from jax.experimental import pallas as pl
from jax.experimental.pallas import tpu as pltpu
from jax.sharding import PartitionSpec as P

F = 672
BS = 640
COLS = 32
SCALE = 1.4426950408889634 / (0.09 * F)
MESH = pl.DeviceIdType.MESH
NT = (((1,), (1,)), ((), ()))
TN = (((0,), (0,)), ((), ()))
F32 = jnp.float32
BF16 = jnp.bfloat16

OWN, X1, X2, Z1, Z2, Y1, Y2, SIB, DG, YN = range(10)
TAB_Z, TAB_X, TAB_D, TAB_Y, TAB_S = range(10, 15)
SLOTS = 10
HEAD, REST, SUB, SQ, TAB = range(5)
BULK, SMALL = (HEAD, REST), (TAB, SQ, SUB)
HALF = 352
CUT = 512

STEPS = [
    ((0, 0), (0, 0)),
    ((0, 1), (0, 3)),
    ((1, 3), (0, 5)),
    ((7, 5), (0, 7)),
    ((0, 6), (0, 0)),
]
COL_PAIRS = ((2, 1), (3, 0), (3, 1), (4, 0))
LAST_STEPS = [
    ((1, 4), (2, 3)),
    ((0, 2), (0, 4)),
]


def pick(index, values):
    result = values[-1]
    for position in range(len(values) - 2, -1, -1):
        result = jnp.where(index == position, values[position], result)
    return result


def item_kernel(hist, basis, row_table, col_table, out, X, B, Q, T, ACC, BACK, RET, STA, STB, STC, STE, G, RT, CT,
                in_sem, send_sem, recv_sem, back_send, back_recv):
    r = lax.axis_index("row")
    c = lax.axis_index("col")
    z, x, y, k = r // 4, lax.rem(r, 4), c // 2, lax.rem(c, 2)
    s = 1 - 2 * k

    def row_at(dx, dz):
        return lax.rem(z + s * dz + 8, 4) * 4 + lax.rem(x + s * dx + 8, 4)

    def col_at(dy):
        return lax.rem(y + s * dy + 8, 4) * 2 + k

    def on_row(dx, dz):
        return (row_at(dx, dz), c)

    def on_col(dy):
        return (r, col_at(dy))

    sibling = (r, y * 2 + 1 - k)
    cross = (r, lax.rem(y + s + 4, 4) * 2 + 1 - k)
    sib_next_col = lax.rem(y + 2, 4) * 2 + 1 - k
    sib_owner_col = jnp.where(k == 0, cross[1], sibling[1])

    barrier = pltpu.get_barrier_semaphore()
    sources = [on_row(-1, 0), on_row(0, -1), on_col(-1), sibling]
    for source in sources:
        pl.semaphore_signal(barrier, inc=1, device_id=source, device_id_type=MESH)

    copies_in = [pltpu.make_async_copy(hist.at[b], X.at[OWN, b], in_sem.at[b]) for b in range(2)]
    copies_in.append(pltpu.make_async_copy(basis, B.at[OWN], in_sem.at[2]))
    tables_in = [pltpu.make_async_copy(row_table, RT, in_sem.at[3]), pltpu.make_async_copy(col_table, CT, in_sem.at[4])]
    for item in tables_in + copies_in:
        item.start()

    ACC[...] = jnp.zeros_like(ACC)

    for item in tables_in:
        item.wait()

    def load_table(i, carry):
        T[OWN, 2 * i] = RT[0, 0, i]
        T[OWN, 2 * i + 1] = RT[0, 1, i]
        return carry

    lax.fori_loop(0, 16, load_table, 0)

    def load_col(i, carry):
        T[OWN, 32 + 2 * i] = CT[0, 0, i]
        T[OWN, 33 + 2 * i] = CT[0, 1, i]
        return carry

    lax.fori_loop(0, 8, load_col, 0)

    for item in copies_in:
        item.wait()
    for b in range(2):
        values = X[OWN, b].astype(F32)
        Q[OWN, b:b + 1] = jnp.sum(values * values, axis=0, keepdims=True) * (-SCALE)

    pl.semaphore_wait(barrier, len(sources))

    def remote(src, dst, send, recv, device):
        return pltpu.make_async_remote_copy(src_ref=src, dst_ref=dst, send_sem=send, recv_sem=recv,
                                            device_id=device, device_id_type=MESH)

    def part(kind, slot):
        if kind in BULK:
            return X.at[slot, :, pl.ds(0, CUT) if kind == HEAD else pl.ds(CUT, F - CUT)]
        return {SUB: B, SQ: Q, TAB: T}[kind].at[slot]

    def copy(path, kind, src, dst, device):
        return remote(part(kind, src), part(kind, dst), send_sem.at[path, kind], recv_sem.at[dst, kind], device)

    def arrived(kind, slot):
        copy(0, kind, slot, slot, sibling).wait_recv()

    paths = [(0, OWN, X1, on_row(1, 0)), (1, OWN, Z1, on_row(0, 1)), (2, OWN, Y1, on_col(1)),
             (4, X1, X2, on_row(1, 0)), (5, Z1, Z2, on_row(0, 1)), (6, Y1, Y2, on_col(1))]

    def send_own(kind):
        for path in paths[:3]:
            copy(path[0], kind, *path[1:]).start()

        @pl.when(k == 0)
        def _():
            copy(3, kind, OWN, SIB, sibling).start()

    for kind in SMALL + (HEAD,):
        send_own(kind)

    def row_of(slot):
        return pick(slot, [r, row_at(-1, 0), row_at(-2, 0), row_at(0, -1), row_at(0, -2), r, r, r, row_at(-1, -1), r])

    def col_of(slot):
        return pick(slot, [c, c, c, c, c, col_at(-1), col_at(-2), sib_owner_col, c, col_at(1)])

    def chosen(i, j, ki, kj):
        return jnp.maximum(T[i, kj], T[j, ki + 1]), jnp.maximum(T[i, kj + 1], T[j, ki])

    def stage_a():
        target, owner = 2 * row_at(0, 1), 2 * row_at(-1, 0)
        return jnp.maximum(T[X1, target], T[TAB_Z, owner + 1])

    def stage_b():
        target, owner = 2 * row_at(1, 0), 2 * row_at(0, -1)
        return jnp.maximum(T[Z1, target], T[TAB_X, owner + 1])

    def stage_cross():
        return jnp.maximum(T[Y1, 32 + 2 * sib_next_col], T[TAB_S, 33 + 2 * col_at(-1)])

    def stage_far():
        return jnp.maximum(T[Y1, 32 + 2 * col_at(1)], T[TAB_Y, 33 + 2 * col_at(-1)])

    def stage_back():
        return jnp.maximum(T[OWN, 32 + 2 * col_at(-2)], T[Y2, 33 + 2 * c])

    def second_y():
        return remote(STC.at[0], X.at[Y2, 0], send_sem.at[6, HEAD], recv_sem.at[Y2, HEAD], on_col(1))

    def next_y():
        return [copy(13, kind, OWN, YN, on_col(-1)) for kind in SMALL] + [
            remote(STC.at[1], X.at[YN, 0], send_sem.at[13, HEAD], recv_sem.at[YN, HEAD], on_col(-1))]

    def sibling_table():
        return remote(T.at[Y2], T.at[TAB_S], send_sem.at[12, TAB], recv_sem.at[TAB_S, TAB], sibling)

    to_z, to_x = on_row(0, 1), on_row(1, 0)

    def diagonal_copies():
        return [
            copy(7, TAB, X1, DG, to_z),
            copy(7, SQ, X1, DG, to_z),
            remote(STE, B.at[DG, 0], send_sem.at[8, SUB], recv_sem.at[DG, SUB], to_x),
            remote(STA.at[pl.ds(0, 256)], X.at[DG, 0, pl.ds(0, 256)], send_sem.at[7, HEAD], recv_sem.at[DG, HEAD], to_z),
            remote(STB.at[pl.ds(64, 256)], X.at[DG, 0, pl.ds(416, 256)], send_sem.at[8, REST], recv_sem.at[DG, REST], to_x),
            remote(STA.at[pl.ds(256, 96)], X.at[DG, 0, pl.ds(256, 96)], send_sem.at[14, HEAD], recv_sem.at[TAB_Z, HEAD], to_z),
            remote(STB.at[pl.ds(0, 64)], X.at[DG, 0, pl.ds(352, 64)], send_sem.at[14, REST], recv_sem.at[TAB_Z, REST], to_x),
        ]

    owners = [None, on_row(-1, 0), on_row(-2, 0), on_row(0, -1), on_row(0, -2), on_col(-1), on_col(-2),
              (r, sib_owner_col), on_row(-1, -1), on_col(1)]

    def give_back(slot):
        part = (slot - 1, 0) if slot == DG else slot - 1
        return remote(BACK.at[part], RET.at[part], back_send.at[slot - 1], back_recv.at[slot - 1], owners[slot])

    def table_back():
        return remote(T.at[OWN], T.at[TAB_D], send_sem.at[7, REST], recv_sem.at[TAB_D, TAB], owners[DG])

    def start_back(slot):
        BACK[slot - 1] = ACC[slot].astype(BF16)
        give_back(slot).start()

    west = x < 2

    def takes(dy):
        return ((z < 2) == (lax.rem(y + s * dy + 4, 4) < 2)) == (k == 1)

    takes_y, next_takes, last_takes = takes(0), takes(1), takes(-1)

    def pair_of(step, place):
        i, j = [pick(step, [entry[place][side] for entry in STEPS]) for side in range(2)]
        along_col = step < 0
        for s_col, p_col in COL_PAIRS:
            if p_col == place:
                along_col = jnp.logical_or(along_col, step == s_col)
        if place == 0:
            swap = jnp.logical_and(step == 4, k == 0)
            i, j = jnp.where(swap, Y1, i), jnp.where(swap, YN, j)
        else:
            swap = jnp.logical_and(step == 3, k == 0)
            i, j = jnp.where(swap, SIB, i), jnp.where(swap, Y2, j)
        ki = jnp.where(along_col, 32 + 2 * col_of(i), 2 * row_of(i))
        kj = jnp.where(along_col, 32 + 2 * col_of(j), 2 * row_of(j))
        bi, bj = chosen(i, j, ki, kj)
        diagonal = step == 0
        bi, bj = jnp.where(diagonal, place, bi), jnp.where(diagonal, place, bj)
        if place == 1:
            bi, bj = jnp.where(step == 4, -1, bi), jnp.where(step == 4, -1, bj)
        at = jnp.where(jnp.logical_or(j == Y2, j == YN), 0, bj)
        return i, j, bi, bj, at

    def last_pair_of(step, place):
        i, j = [pick(step, [entry[place][side] for entry in LAST_STEPS]) for side in range(2)]
        if place == 0:
            swap = jnp.logical_and(step == 1, jnp.logical_not(west))
            i, j = jnp.where(swap, X2, i), jnp.where(swap, Z2, j)
        bi, bj = chosen(i, j, 2 * row_of(i), 2 * row_of(j))
        if place == 1:
            left_out = jnp.logical_and(step == 1, takes_y)
            bi, bj = jnp.where(left_out, -1, bi), jnp.where(left_out, -1, bj)
        return i, j, bi, bj, bj

    def inner_of(i, j, bi, at, rows):
        left = jnp.where(bi == 0, X[i, 0, rows], X[i, 1, rows])
        right = X[j, at, rows] if isinstance(at, int) else jnp.where(at == 0, X[j, 0, rows], X[j, 1, rows])
        return lax.dot_general(left, right, TN, preferred_element_type=F32)

    def kernel_of(inner, i, j, bi, bj):
        left_squares = jnp.where(bi == 0, Q[i, 0:1], Q[i, 1:2])
        right_squares = jnp.where(bj == 0, Q[j, 0:1], Q[j, 1:2])
        squares = jnp.broadcast_to(left_squares, (8, BS)).T[:, 0:1] + right_squares
        return jnp.exp2(jnp.minimum(inner * (2 * SCALE) + squares, 0.0)).astype(BF16)

    def tile(i, j, bi, bj, at):
        return kernel_of(inner_of(i, j, bi, at, slice(None)), i, j, bi, bj)

    def add_terms(pairs, kernels, diagonal):
        for (i, j, bi, bj, _), kernel in zip(pairs, kernels):
            for_left, for_right = left_part(kernel, j, bj), right_part(kernel, i, bi)
            for b in range(2):
                ACC[i, b] += jnp.where(jnp.logical_and(bi == b, jnp.logical_not(diagonal)), for_left, 0.0)
                ACC[j, b] += jnp.where(bj == b, for_right, 0.0)

    def left_part(kernel, j, bj):
        right_basis = jnp.where(bj == 0, B[j, 0], B[j, 1])
        return lax.dot_general(kernel, right_basis, NT, preferred_element_type=F32).T

    def right_part(kernel, i, bi):
        return jnp.dot(jnp.where(bi == 0, B[i, 0], B[i, 1]), kernel, preferred_element_type=F32)

    def step_body(step, carry):
        @pl.when(step == 0)
        def _():
            for slot in (X1, Z1, Y1):
                for kind in SMALL:
                    arrived(kind, slot)
            copy(9, TAB, OWN, TAB_Z, on_row(0, -1)).start()
            copy(10, TAB, OWN, TAB_X, on_row(-1, 0)).start()
            copy(11, TAB, OWN, TAB_Y, on_col(-1)).start()
            for kind in SMALL:
                for path in paths[3:]:
                    copy(path[0], kind, *path[1:]).start()

                @pl.when(k == 1)
                def _():
                    copy(3, kind, Y1, SIB, sibling).start()

            send_own(REST)

            @pl.when(k == 1)
            def _():
                arrived(TAB, Y2)
                sibling_table().start()

            for kind in BULK:
                for slot, path in zip((X1, Z1), paths[3:]):
                    arrived(kind, slot)
                    copy(path[0], kind, *path[1:]).start()
                arrived(kind, Y1)

                @pl.when(k == 1)
                def _():
                    copy(3, kind, Y1, SIB, sibling).start()
            arrived(TAB, TAB_Y)

            @pl.when(k == 0)
            def _():
                arrived(TAB, TAB_S)
                STC[0] = jnp.where(stage_cross() == 0, X[Y1, 0], X[Y1, 1])
                second_y().start()

            @pl.when(k == 0)
            def _():
                arrived(TAB, Y2)

            @pl.when(jnp.logical_and(k == 0, last_takes))
            def _():
                STC[1] = jnp.where(stage_back() == 0, X[OWN, 0], X[OWN, 1])
                for item in next_y():
                    item.start()

            @pl.when(jnp.logical_and(k == 1, next_takes))
            def _():
                STC[0] = jnp.where(stage_far() == 0, X[Y1, 0], X[Y1, 1])
                second_y().start()

            arrived(TAB, TAB_Z)
            arrived(TAB, TAB_X)
            STA[...] = jnp.where(stage_a() == 0, X[X1, 0, 0:HALF], X[X1, 1, 0:HALF])
            STB[...] = jnp.where(stage_b() == 0, X[Z1, 0, HALF:F], X[Z1, 1, HALF:F])
            STE[...] = jnp.where(stage_b() == 0, B[Z1, 0], B[Z1, 1])
            for item in diagonal_copies():
                item.start()

        @pl.when(step == 3)
        def _():
            arrived(TAB, X2)
            table_back().start()
            for kind in SMALL + BULK:
                arrived(kind, SIB)

            @pl.when(k == 0)
            def _():
                second_y().wait_recv()

            for kind in (SQ, SUB):
                arrived(kind, Y2)

        @pl.when(jnp.logical_and(step == 4, k == 0))
        def _():
            for item in next_y():
                item.wait_recv()

        @pl.when(jnp.logical_and(step == 4, k == 1))
        def _():
            second_y().wait_recv()

        pairs = [pair_of(step, place) for place in range(2)]
        add_terms(pairs, [tile(*pair) for pair in pairs], step == 0)
        return carry

    lax.fori_loop(0, len(STEPS) - 1 + takes_y.astype(jnp.int32), step_body, 0)
    for slot in (Y1, SIB, Y2):
        start_back(slot)
    for path in paths:
        for kind in SMALL if path[0] >= 4 else SMALL + BULK:
            copy(path[0], kind, *path[1:]).wait_send()

    @pl.when(jnp.logical_or(k == 0, next_takes))
    def _():
        second_y().wait_send()

    @pl.when(jnp.logical_and(k == 0, last_takes))
    def _():
        for item in next_y():
            item.wait_send()

    @pl.when(k == 1)
    def _():
        sibling_table().wait_send()

    for kind in SMALL + BULK:
        copy(3, kind, OWN, SIB, sibling).wait_send()
    copy(9, TAB, OWN, TAB_Z, on_row(0, -1)).wait_send()
    copy(10, TAB, OWN, TAB_X, on_row(-1, 0)).wait_send()
    copy(11, TAB, OWN, TAB_Y, on_col(-1)).wait_send()

    @pl.when(jnp.logical_and(k == 0, takes_y))
    def _():
        start_back(YN)

    for slot, kinds in ((X2, (SQ, SUB, HEAD)), (Z2, SMALL + (HEAD,))):
        for kind in kinds:
            arrived(kind, slot)
    head, rest = slice(0, CUT), slice(CUT, F)

    def early_body(step, carry):
        for place in range(2):
            i, j, bi, _, at = last_pair_of(step, place)
            G[2 * step + place] = inner_of(i, j, bi, at, head)
        return carry

    lax.fori_loop(0, len(LAST_STEPS), early_body, 0)
    for slot in (X2, Z2):
        arrived(REST, slot)

    def last_body(step, carry):
        pairs = [last_pair_of(step, place) for place in range(2)]
        kernels = []
        for place, (i, j, bi, bj, at) in enumerate(pairs):
            kernels.append(kernel_of(G[2 * step + place] + inner_of(i, j, bi, at, rest), i, j, bi, bj))
        add_terms(pairs, kernels, False)

        @pl.when(step == 0)
        def _():
            start_back(X1)
            start_back(Z1)

        return carry

    lax.fori_loop(0, len(LAST_STEPS), last_body, 0)
    start_back(X2)
    start_back(Z2)
    diagonal_parts = diagonal_copies()
    for item in diagonal_parts[:-2]:
        item.wait_recv()
    bi, bj = chosen(OWN, DG, 2 * r, 2 * row_at(-1, -1))
    G[0] = inner_of(OWN, DG, bi, 0, slice(0, 256)) + inner_of(OWN, DG, bi, 0, slice(416, F))
    for item in diagonal_parts[-2:]:
        item.wait_recv()
    kernel = kernel_of(G[0] + inner_of(OWN, DG, bi, 0, slice(256, 416)), OWN, DG, bi, bj)
    BACK[DG - 1, 0] = jnp.where(bj >= 0, right_part(kernel, OWN, bi), 0.0).astype(BF16)
    give_back(DG).start()
    for_left = left_part(kernel, DG, 0)
    total = [ACC[OWN, b] + jnp.where(bi == b, for_left, 0.0) for b in range(2)]

    for path in paths[3:5]:
        for kind in BULK:
            copy(path[0], kind, *path[1:]).wait_send()
    for item in diagonal_copies():
        item.wait_send()
    for slot in (Y1, X1, Z1, X2, SIB, Y2, Z2):
        give_back(slot).wait()
        for b in range(2):
            total[b] = total[b] + RET[slot - 1, b].astype(F32)

    @pl.when(jnp.logical_and(k == 0, takes_y))
    def _():
        give_back(YN).wait_send()

    given = jnp.logical_and(k == 0, last_takes)

    @pl.when(given)
    def _():
        give_back(YN).wait_recv()

    @pl.when(jnp.logical_not(given))
    def _():
        RET[YN - 1] = jnp.zeros((2, COLS, BS), BF16)

    total = [total[b] + RET[YN - 1, b].astype(F32) for b in range(2)]
    table_back().wait()
    mine = jnp.maximum(T[OWN, 2 * row_at(1, 1)], T[TAB_D, 2 * r + 1])
    give_back(DG).wait()
    last = RET[DG - 1, 0].astype(F32)
    for b in range(2):
        out[b] = total[b] + jnp.where(mine == b, last, 0.0)


def body(histograms, basis, row_pairs, col_pairs):
    return pl.pallas_call(
        item_kernel,
        out_shape=jax.ShapeDtypeStruct((2, COLS, BS), F32),
        in_specs=[
            pl.BlockSpec(memory_space=pl.ANY),
            pl.BlockSpec(memory_space=pl.ANY),
            pl.BlockSpec(memory_space=pl.ANY),
            pl.BlockSpec(memory_space=pl.ANY),
        ],
        out_specs=pl.BlockSpec(memory_space=pltpu.VMEM),
        scratch_shapes=[
            pltpu.VMEM((SLOTS, 2, F, BS), BF16),
            pltpu.VMEM((SLOTS, 2, COLS, BS), BF16),
            pltpu.VMEM((SLOTS, 2, BS), F32),
            pltpu.SMEM((15, 48), jnp.int32),
            pltpu.VMEM((SLOTS, 2, COLS, BS), F32),
            pltpu.VMEM((SLOTS - 1, 2, COLS, BS), BF16),
            pltpu.VMEM((SLOTS - 1, 2, COLS, BS), BF16),
            pltpu.VMEM((HALF, BS), BF16),
            pltpu.VMEM((F - HALF, BS), BF16),
            pltpu.VMEM((2, F, BS), BF16),
            pltpu.VMEM((COLS, BS), BF16),
            pltpu.VMEM((4, BS, BS), F32),
            pltpu.SMEM((1, 2, 16), jnp.int32),
            pltpu.SMEM((1, 2, 8), jnp.int32),
            pltpu.SemaphoreType.DMA((5,)),
            pltpu.SemaphoreType.DMA((15, 5)),
            pltpu.SemaphoreType.DMA((15, 5)),
            pltpu.SemaphoreType.DMA((SLOTS - 1,)),
            pltpu.SemaphoreType.DMA((SLOTS - 1,)),
        ],
        compiler_params=pltpu.CompilerParams(
            collective_id=0, has_side_effects=True, vmem_limit_bytes=56 * 1024 * 1024
        ),
    )(jnp.swapaxes(histograms, 1, 2), basis, jnp.swapaxes(row_pairs, 1, 2), jnp.swapaxes(col_pairs, 1, 2))


def solution(mesh):
    spec = P(("row", "col"), None, None)
    return jax.shard_map(body, mesh=mesh, in_specs=(spec,) * 4, out_specs=spec, check_vma=False)
```
